32 devices in a mesh: grp: 2 (over x), exp: 16 (over z, y, core).
Axes of the slice: x: 2, y: 2, z: 4, core: 2. Of those that a mesh axis runs over, the one named last changes fastest.
Arguments:
- queries: bfloat16 [64, 128, 576], P(('grp', 'exp')), parts along dimension 0, may hold values from -18 to 18
- latent_key_cache: bfloat16 [64, 2048, 576], P(('grp', 'exp')), parts along dimension 0, may hold values from -5 to 5
- lengths: int32 [64], P(('grp', 'exp')), parts along dimension 0, may hold values from 2 to 2048, as said below
- value_up_weight: bfloat16 [128, 512, 128], P('exp'), may hold values from -0.75 to 0.75
- out_proj: bfloat16 [16384, 7168], P('exp'), may hold values from -0.1875 to 0.1875
- residual_in: bfloat16 [64, 7168], P(('grp', 'exp')), parts along dimension 0, may hold values from -45 to 45
- norm_gain: float32 [7168], replicated, may hold values from 0.5 to 1.5
- w_gate: bfloat16 [7168, 16384], P(None, 'exp'), may hold values from -0.0625 to 0.0625
- w_up: bfloat16 [7168, 16384], P(None, 'exp'), may hold values from -0.0625 to 0.0625
- w_down: bfloat16 [16384, 7168], P('exp'), may hold values from -0.1875 to 0.1875
- routes: int32 [64, 8], P(('grp', 'exp')), parts along dimension 0, may hold values from 0 to 15, all different within a row
- route_gates: float32 [64, 8], P(('grp', 'exp')), parts along dimension 0, may hold values from 0.05 to 0.6
Outputs:
- attended: bfloat16 [64, 7168], P(('grp', 'exp')), parts along dimension 0
- expert_mix: bfloat16 [64, 7168], P(('grp', 'exp')), parts along dimension 0
The draws below stay inside these ranges and needn't reach their ends.
There are 2 independent parts, one for each index of `grp`. The reference program is written for one: setup_inputs(seed, part) draws one part's arguments, and reference() takes and returns one part's arrays. A program takes and returns all parts, laid end to end along the dimension named above; an argument that names none is the same for every part. Nothing has to cross between parts.
Inputs may be any that keep to these rules, and one draw needn't show every extreme that they name: `lengths`: one request of every draw holds 2048 cached positions. `routes`: each row names 8 different experts.
All inputs are finite; a program needn't handle non-finite values.
Results may differ from the reference program's by a relative error of at most 0.013.
Values may be sent and summed in bfloat16 or wider, within the bound.
No kernel may reach another device: no remote copies, remote signals or barrier semaphores. Data moves between devices by JAX's collectives and lax.ppermute only.
A program may use at most 192 MiB of HBM per device.

```python
import math
import jax
import jax.numpy as jnp
from jax import lax

D = 7168
HEAD_TOTAL = 128
LATENT_WIDTH = 512
ROTARY_WIDTH = 64
HEAD_VALUE_WIDTH = 128
TOP = 8
FF_WIN = 1024
EXPERTS = 16
CACHE_CAPACITY = 2048
REQUEST_TOTAL = 32
PIECE = 1024


def draw_latent_key_cache(key, part):
    key = jax.random.fold_in(key, 1)
    starting_values = jnp.clip(jax.random.normal(key, (REQUEST_TOTAL, CACHE_CAPACITY, LATENT_WIDTH + ROTARY_WIDTH), jnp.float32), -5.0, 5.0)
    return starting_values.astype(jnp.bfloat16)


def draw_queries(key, part):
    key = jax.random.fold_in(key, 2)
    starting_values = jnp.clip(jax.random.normal(key, (REQUEST_TOTAL, HEAD_TOTAL, LATENT_WIDTH + ROTARY_WIDTH), jnp.float32), -5.0, 5.0)
    return starting_values.astype(jnp.bfloat16)


def draw_lengths(key, part):
    key = jax.random.fold_in(key, 3)
    drawn_lengths = jax.random.randint(key, (REQUEST_TOTAL,), 2, CACHE_CAPACITY + 1)
    return drawn_lengths.at[0].set(CACHE_CAPACITY).astype(jnp.int32)


def draw_residual_in(key, part):
    key = jax.random.fold_in(key, 4)
    row_scale = jnp.exp(jax.random.uniform(jax.random.fold_in(key, 5), (REQUEST_TOTAL, 1), jnp.float32, math.log(0.3), math.log(3.0)))
    column_scale = jnp.exp(jax.random.uniform(jax.random.fold_in(key, 6), (1, D), jnp.float32, math.log(0.3), math.log(3.0)))
    starting_values = jnp.clip(jax.random.normal(key, (REQUEST_TOTAL, D), jnp.float32), -5.0, 5.0)
    return (starting_values * row_scale * column_scale).astype(jnp.bfloat16)


def block_scale(own_key, extent, shards, least, top_value):
    gain = 1.0
    for axis_at, blocks in shards:
        draws = jax.random.uniform(jax.random.fold_in(jax.random.fold_in(own_key, 6), axis_at), (blocks,), jnp.float32, least / len(shards), top_value / len(shards))
        gain = gain * jnp.repeat(jnp.exp(draws), extent[axis_at] // blocks).reshape((-1,) + (1,) * (len(extent) - 1 - axis_at))
    return gain


def picks_of(rng, rows, number_of, top, lift):
    sequence = jax.random.permutation(jax.random.fold_in(rng, 1), number_of)
    boost = sequence
    for power in range(3):
        boost = boost * boost // number_of
    boost = boost * lift // number_of
    lots = jax.random.randint(jax.random.fold_in(rng, 2), (rows, number_of), 0, 4096) + boost
    holders = jax.random.permutation(jax.random.fold_in(rng, 3), rows)[jnp.arange(number_of) % rows]
    lots = jnp.where(jnp.arange(rows)[:, None] == holders[None, :], 1 << 14, lots)
    priority = lots * number_of + jnp.arange(number_of)
    return lax.top_k(priority.astype(jnp.int32), top)[1].astype(jnp.int32)


def noise(own_key, dims, scale, limit, pieces=(), kind=jnp.bfloat16):
    values = jax.random.normal(own_key, dims, jnp.float32) * scale
    if len(pieces) > 0:
        values = block_scale(own_key, dims, pieces, -0.22, 0.18) * values
    return jnp.clip(values, min=-limit, max=limit).astype(kind)


def setup_inputs(seed: int = 0, part: int = 0) -> dict:
    key_list = jax.random.split(jax.random.key(seed), 13)
    part_keys = jax.random.split(jax.random.fold_in(key_list[12], part), 13)
    return {
        "queries": draw_queries(jax.random.fold_in(jax.random.fold_in(key_list[12], part), 71), part),
        "latent_key_cache": draw_latent_key_cache(jax.random.fold_in(jax.random.fold_in(key_list[12], part), 71), part),
        "lengths": draw_lengths(jax.random.fold_in(jax.random.fold_in(key_list[12], part), 71), part),
        "value_up_weight": noise(key_list[3], (HEAD_TOTAL, LATENT_WIDTH, HEAD_VALUE_WIDTH), (LATENT_WIDTH // 8) ** -0.5, 0.75, ((0, 16),)),
        "out_proj": noise(key_list[4], (HEAD_TOTAL * HEAD_VALUE_WIDTH, D), (HEAD_TOTAL * HEAD_VALUE_WIDTH // 16) ** -0.5, 0.1875, ((0, 16),)),
        "residual_in": draw_residual_in(jax.random.fold_in(jax.random.fold_in(key_list[12], part), 71), part),
        "norm_gain": jnp.clip(1.0 + 0.1 * jax.random.normal(key_list[6], (D,), jnp.float32), 0.5, 1.5),
        "w_gate": noise(key_list[7], (D, EXPERTS * FF_WIN), D ** -0.5, 0.0625, ((1, 16),)),
        "w_up": noise(key_list[8], (D, EXPERTS * FF_WIN), D ** -0.5, 0.0625, ((1, 16),)),
        "w_down": noise(key_list[9], (EXPERTS * FF_WIN, D), FF_WIN ** -0.5, 0.1875, ((0, 16),)),
        "routes": picks_of(part_keys[10], REQUEST_TOTAL, EXPERTS, TOP, 8192),
        "route_gates": jnp.clip(0.05 + 0.55 * jax.random.uniform(part_keys[11], (REQUEST_TOTAL, TOP), jnp.float32) ** block_scale(part_keys[11], (REQUEST_TOTAL, TOP), ((0, 16),), -0.2, 0.2), 0.05, 0.6),
    }


def reference(queries, latent_key_cache, lengths, value_up_weight, out_proj, residual_in, norm_gain, w_gate, w_up, w_down, routes, route_gates):
    score_scale = (HEAD_VALUE_WIDTH + ROTARY_WIDTH) ** (-0.5)

    def one_request(operands):
        query_rows, cache_row_set, length_now = operands
        scores = jnp.einsum('hc,jc->hj', query_rows.astype(jnp.float32), cache_row_set.astype(jnp.float32)) * score_scale
        visible = jnp.arange(CACHE_CAPACITY, dtype=jnp.int32) < length_now
        scores = jnp.where(visible[None, :], scores, -jnp.inf)
        peak_score = lax.optimization_barrier(jnp.max(scores, axis=1, keepdims=True))
        exponent = jnp.exp(scores - peak_score)
        probabilities = (exponent / lax.optimization_barrier(jnp.sum(exponent, axis=1, keepdims=True))).astype(jnp.bfloat16)
        latent_row_set = cache_row_set[:, :LATENT_WIDTH].astype(jnp.float32)
        return jnp.einsum('hj,jc->hc', probabilities.astype(jnp.float32), latent_row_set).astype(jnp.bfloat16)
    latent_out = lax.map(one_request, (queries, latent_key_cache, lengths))
    head_values = jnp.einsum('rhc,hcv->rhv', latent_out.astype(jnp.float32), value_up_weight.astype(jnp.float32)).astype(jnp.bfloat16)
    attention_sum = jnp.dot(head_values.reshape(REQUEST_TOTAL, HEAD_TOTAL * HEAD_VALUE_WIDTH), out_proj, preferred_element_type=jnp.float32)
    attended = (residual_in.astype(jnp.float32) + attention_sum).astype(jnp.bfloat16)
    attended_wide = attended.astype(jnp.float32)
    normed = (attended_wide * lax.rsqrt(lax.optimization_barrier(jnp.mean(attended_wide * attended_wide, axis=1, keepdims=True)) + 1e-06) * norm_gain.astype(jnp.float32)).astype(jnp.bfloat16)
    matches = routes[:, :, None] == jnp.arange(EXPERTS, dtype=jnp.int32)[None, None, :]
    gate_table = lax.optimization_barrier(jnp.sum(jnp.where(matches, route_gates.astype(jnp.float32)[:, :, None], 0.0), axis=1))
    piece_count = FF_WIN // PIECE

    def expert_step(running_sum, expert_id):
        first_unit = (expert_id * FF_WIN).astype(jnp.int32)
        gate_cols = lax.dynamic_slice_in_dim(w_gate, first_unit, FF_WIN, 1)
        up_cols = lax.dynamic_slice_in_dim(w_up, first_unit, FF_WIN, 1)
        down_rows = lax.dynamic_slice_in_dim(w_down, first_unit, FF_WIN, 0)
        gate_part = jnp.dot(normed, gate_cols, preferred_element_type=jnp.float32)
        up_part = jnp.dot(normed, up_cols, preferred_element_type=jnp.float32)
        activation = (jax.nn.silu(gate_part) * up_part).astype(jnp.bfloat16)
        activation_pieces = activation.reshape(REQUEST_TOTAL, piece_count, PIECE).astype(jnp.float32)
        down_pieces = down_rows.reshape(piece_count, PIECE, D).astype(jnp.float32)
        piece_outputs = jnp.einsum('rnp,npd->rnd', activation_pieces, down_pieces).astype(jnp.bfloat16)
        expert_output = lax.optimization_barrier(jnp.sum(piece_outputs.astype(jnp.float32), axis=1))
        gate_column = lax.dynamic_slice_in_dim(gate_table, expert_id, 1, 1)
        return (running_sum + gate_column * expert_output, None)
    expert_sum, _ = lax.scan(expert_step, jnp.zeros((REQUEST_TOTAL, D), jnp.float32), jnp.arange(EXPERTS, dtype=jnp.int32))
    return (attended, expert_sum.astype(jnp.bfloat16))
```

```python
import functools

import jax
import jax.numpy as jnp
from jax import lax
from jax.experimental import pallas as pl
from jax.experimental.pallas import tpu as pltpu
from jax.sharding import PartitionSpec as P

LATENT_WIDTH = 512
ROTARY_WIDTH = 64
HEAD_VALUE_WIDTH = 128
FF_WIN = 1024
MIB = 1 << 20


def tile_of(extent, wanted):
    while extent % wanted:
        wanted //= 2
    return wanted


def attend_kernel(lengths_ref, q_ref, cache_hbm, out_ref, cache, sems):
    requests, width, length = cache.shape
    chunk = tile_of(length, 512)
    chunks = length // chunk
    devices, slots, latent = out_ref.shape
    heads = slots // requests
    scale = (HEAD_VALUE_WIDTH + ROTARY_WIDTH) ** (-0.5)

    def copy(r, c):
        at = pl.ds(c * chunk, chunk)
        return pltpu.make_async_copy(
            cache_hbm.at[r, :, at], cache.at[r, :, at], sems.at[r, c]
        )

    for r in range(requests):
        for c in range(chunks):
            copy(r, c).start()
    results = []
    for r in range(requests):
        q = q_ref[r].astype(jnp.float32).T.astype(jnp.bfloat16)
        scores = []
        for c in range(chunks):
            copy(r, c).wait()
            s = jnp.dot(
                q,
                cache[r, :, c * chunk : (c + 1) * chunk],
                preferred_element_type=jnp.float32,
            )
            at = lax.broadcasted_iota(jnp.int32, s.shape, 1) + c * chunk
            scores.append(jnp.where(at < lengths_ref[r], s * scale, -jnp.inf))
        scores = jnp.concatenate(scores, axis=1)
        peak = jnp.max(scores, axis=1, keepdims=True)
        e = jnp.exp(scores - peak)
        p = (e / jnp.sum(e, axis=1, keepdims=True)).astype(jnp.bfloat16)
        o = lax.dot_general(
            p,
            cache[r, :latent, :],
            (((1,), (1,)), ((), ())),
            preferred_element_type=jnp.float32,
        )
        results.append(o.reshape(devices, heads, latent))
    out_ref[...] = jnp.concatenate(results, axis=1).astype(out_ref.dtype)


def attend(queries, cache, lengths, devices):
    requests, heads, width = queries.shape
    length = cache.shape[1]
    slots = requests * heads // devices
    chunks = length // tile_of(length, 512)
    return pl.pallas_call(
        attend_kernel,
        out_shape=jax.ShapeDtypeStruct((devices, slots, LATENT_WIDTH), jnp.bfloat16),
        in_specs=[
            pl.BlockSpec(memory_space=pltpu.SMEM),
            pl.BlockSpec(memory_space=pltpu.VMEM),
            pl.BlockSpec(memory_space=pl.ANY),
        ],
        out_specs=pl.BlockSpec(memory_space=pltpu.VMEM),
        scratch_shapes=[
            pltpu.VMEM((requests, width, length), jnp.bfloat16),
            pltpu.SemaphoreType.DMA((requests, chunks)),
        ],
        compiler_params=pltpu.CompilerParams(vmem_limit_bytes=24 * MIB),
        name="attend",
    )(lengths, jnp.swapaxes(queries, 1, 2), jnp.swapaxes(cache, 1, 2))


def relative(index, bits):
    out = jnp.zeros_like(index)
    for b in range(bits):
        out = out | (((index >> b) & 1) << (bits - 1 - b))
    return out


def row_order(me, rows, per, bits, shape):
    i = lax.broadcasted_iota(jnp.int32, shape, 0)
    j = lax.broadcasted_iota(jnp.int32, shape, 1)
    shift = per.bit_length() - 1
    owner = relative(i >> shift, bits) ^ me
    return j == (owner << shift) + (i & (per - 1))


def project_kernel(bits, per, me_ref, latent_ref, up_ref, proj_hbm, out_ref, proj, sems):
    depth, width = proj.shape
    tiles = sems.shape[0]
    tile = width // tiles
    heads, latent, value = up_ref.shape
    rows = latent_ref.shape[0] // heads

    def copy(t):
        at = pl.ds(t * tile, tile)
        return pltpu.make_async_copy(proj_hbm.at[:, at], proj.at[:, at], sems.at[t])

    for t in range(tiles):
        copy(t).start()
    x = latent_ref[...]
    parts = []
    for h in range(heads):
        y = jnp.dot(x, up_ref[h], preferred_element_type=jnp.float32)
        y = y.reshape(rows, heads, value)
        mine = lax.broadcasted_iota(jnp.int32, y.shape, 1) == h
        parts.append(jnp.sum(jnp.where(mine, y, 0.0), axis=1))
    values = jnp.concatenate(parts, axis=1).astype(jnp.bfloat16)
    order = row_order(me_ref[0], rows, per, bits, (rows, rows))
    order = jnp.where(order, 1.0, 0.0).astype(jnp.bfloat16)
    values = jnp.dot(order, values, preferred_element_type=jnp.float32).astype(jnp.bfloat16)
    for t in range(tiles):
        copy(t).wait()
        out_ref[:, t * tile : (t + 1) * tile] = jnp.dot(
            values, proj[:, t * tile : (t + 1) * tile], preferred_element_type=jnp.float32
        ).astype(out_ref.dtype)


def project(me, latent, up, proj, per, bits):
    depth, width = proj.shape
    rows = latent.shape[0] // up.shape[0]
    tile = tile_of(width, 1024)
    return pl.pallas_call(
        functools.partial(project_kernel, bits, per),
        out_shape=jax.ShapeDtypeStruct((rows, width), jnp.bfloat16),
        in_specs=[
            pl.BlockSpec(memory_space=pltpu.SMEM),
            pl.BlockSpec(memory_space=pltpu.VMEM),
            pl.BlockSpec(memory_space=pltpu.VMEM),
            pl.BlockSpec(memory_space=pl.ANY),
        ],
        out_specs=pl.BlockSpec(memory_space=pltpu.VMEM),
        scratch_shapes=[
            pltpu.VMEM((depth, width), jnp.bfloat16),
            pltpu.SemaphoreType.DMA((width // tile,)),
        ],
        compiler_params=pltpu.CompilerParams(vmem_limit_bytes=32 * MIB),
        name="project",
    )(me, latent, up, proj)


def norm_kernel(kept_ref, came_ref, residual_ref, gain_ref, attended_ref, normed_ref):
    total = (
        residual_ref[...].astype(jnp.float32)
        + kept_ref[...].astype(jnp.float32)
        + came_ref[...].astype(jnp.float32)
    )
    attended = total.astype(jnp.bfloat16)
    attended_ref[...] = attended
    wide = attended.astype(jnp.float32)
    mean = jnp.mean(wide * wide, axis=1, keepdims=True)
    normed_ref[...] = (wide * lax.rsqrt(mean + 1e-06) * gain_ref[...]).astype(jnp.bfloat16)


def add_norm(kept, came, residual, gain):
    shape = jax.ShapeDtypeStruct(residual.shape, jnp.bfloat16)
    return pl.pallas_call(norm_kernel, out_shape=(shape, shape), name="add_norm")(
        kept, came, residual, gain.reshape(1, -1)
    )


def expert_kernel(
    bits, per, me_ref, x_ref, routes_ref, gates_ref, gate_hbm, up_hbm, down_hbm,
    out_ref, gate, up, down, sems,
):
    model, units = gate.shape
    steps = sems.shape[1]
    tile = model // steps
    rows = x_ref.shape[0]
    me = me_ref[0]

    def copies(t):
        at = pl.ds(t * tile, tile)
        return (
            pltpu.make_async_copy(gate_hbm.at[at], gate.at[at], sems.at[0, t]),
            pltpu.make_async_copy(up_hbm.at[at], up.at[at], sems.at[1, t]),
        )

    def down_copy(t):
        at = pl.ds(t * tile, tile)
        return pltpu.make_async_copy(down_hbm.at[:, at], down.at[:, at], sems.at[2, t])

    for t in range(steps):
        for c in copies(t):
            c.start()
    for t in range(steps):
        down_copy(t).start()
    expert = (me * units) // FF_WIN
    weight = jnp.sum(
        jnp.where(routes_ref[...] == expert, gates_ref[...], 0.0), axis=0, keepdims=True
    )
    order = row_order(me, rows, per, bits, (rows, rows))
    weight = jnp.sum(jnp.where(order, weight, 0.0), axis=1, keepdims=True)
    g = jnp.zeros((rows, units), jnp.float32)
    u = jnp.zeros((rows, units), jnp.float32)
    for t in range(steps):
        at = slice(t * tile, (t + 1) * tile)
        x = x_ref[:, at]
        first, second = copies(t)
        first.wait()
        g = g + jnp.dot(x, gate[at], preferred_element_type=jnp.float32)
        second.wait()
        u = u + jnp.dot(x, up[at], preferred_element_type=jnp.float32)
    act = (g / (1.0 + jnp.exp(-g)) * u).astype(jnp.bfloat16)
    for t in range(steps):
        at = slice(t * tile, (t + 1) * tile)
        down_copy(t).wait()
        y = jnp.dot(act, down[:, at], preferred_element_type=jnp.float32)
        out_ref[:, at] = (y * weight).astype(out_ref.dtype)


def experts(me, x, routes, gates, gate, up, down, per, bits):
    model, units = gate.shape
    steps = model // tile_of(model, 1024)
    return pl.pallas_call(
        functools.partial(expert_kernel, bits, per),
        out_shape=jax.ShapeDtypeStruct(x.shape, jnp.bfloat16),
        in_specs=[pl.BlockSpec(memory_space=pltpu.SMEM)]
        + [pl.BlockSpec(memory_space=pltpu.VMEM)] * 3
        + [pl.BlockSpec(memory_space=pl.ANY)] * 3,
        out_specs=pl.BlockSpec(memory_space=pltpu.VMEM),
        scratch_shapes=[
            pltpu.VMEM((model, units), jnp.bfloat16),
            pltpu.VMEM((model, units), jnp.bfloat16),
            pltpu.VMEM((units, model), jnp.bfloat16),
            pltpu.SemaphoreType.DMA((3, steps)),
        ],
        compiler_params=pltpu.CompilerParams(vmem_limit_bytes=56 * MIB),
        name="experts",
    )(me, x, routes, gates, gate, up, down)


def body(
    queries,
    latent_key_cache,
    lengths,
    value_up_weight,
    out_proj,
    residual_in,
    norm_gain,
    w_gate,
    w_up,
    w_down,
    routes,
    route_gates,
):
    devices = lax.axis_size("exp")
    bits = devices.bit_length() - 1
    per = queries.shape[0]
    me = lax.axis_index("exp").astype(jnp.int32).reshape(1)

    def swap(x, bit):
        return lax.ppermute(x, "exp", [(i, i ^ (1 << bit)) for i in range(devices)])

    def add(a, b):
        return (a.astype(jnp.float32) + b.astype(jnp.float32)).astype(jnp.bfloat16)

    def halve(x, stop):
        for bit in range(stop):
            half = x.shape[0] // 2
            x = add(x[:half], swap(x[half:], bit))
        return x

    routes_all = lax.all_gather(jnp.transpose(routes), "exp", axis=1, tiled=True)
    gates_all = lax.all_gather(jnp.transpose(route_gates), "exp", axis=1, tiled=True)

    latent = attend(queries, latent_key_cache, lengths, devices)
    latent = lax.all_to_all(latent, "exp", split_axis=0, concat_axis=0, tiled=True)
    latent = latent.reshape(-1, LATENT_WIDTH)
    part = project(me, latent, value_up_weight, out_proj, per, bits)
    part = halve(part, bits - 1)
    came = swap(part[per:], bits - 1)
    attended, x = add_norm(part[:per], came, residual_in, norm_gain)
    for bit in reversed(range(bits)):
        x = jnp.concatenate([x, swap(x, bit)], axis=0)
    mixed = experts(me, x, routes_all, gates_all, w_gate, w_up, w_down, per, bits)
    mixed = halve(mixed, bits)
    return attended, mixed


def solution(mesh):
    placed = (
        P(("grp", "exp"), None, None),
        P(("grp", "exp"), None, None),
        P(("grp", "exp")),
        P("exp", None, None),
        P("exp", None),
        P(("grp", "exp"), None),
        P(),
        P(None, "exp"),
        P(None, "exp"),
        P("exp", None),
        P(("grp", "exp"), None),
        P(("grp", "exp"), None),
    )
    return jax.shard_map(
        body,
        mesh=mesh,
        in_specs=placed,
        out_specs=(P(("grp", "exp"), None), P(("grp", "exp"), None)),
        check_vma=False,
    )
```

```python
import functools

import jax
import jax.numpy as jnp
from jax import lax
from jax.experimental import pallas as pl
from jax.experimental.pallas import tpu as pltpu
from jax.sharding import PartitionSpec as P

LATENT_WIDTH = 512
ROTARY_WIDTH = 64
HEAD_VALUE_WIDTH = 128
FF_WIN = 1024
TABLE = 128
MIB = 1 << 20

HBM = pl.BlockSpec(memory_space=pl.ANY)
VMEM = pl.BlockSpec(memory_space=pltpu.VMEM)
SMEM = pl.BlockSpec(memory_space=pltpu.SMEM)


def tile_of(extent, wanted):
    while extent % wanted:
        wanted //= 2
    return wanted


def in_hbm(x):
    return pltpu.with_memory_space_constraint(x, pltpu.HBM)


def in_vmem(x):
    return pltpu.with_memory_space_constraint(x, pltpu.VMEM)


TOKEN = pltpu.VMEM((8, 128), jnp.float32)


def call(kernel, name, outs, ins, specs, scratch=(), limit=4, moved=None):
    cost = None
    if moved:
        cost = pl.CostEstimate(flops=0, bytes_accessed=moved, transcendentals=0)
    return pl.pallas_call(
        kernel,
        out_shape=outs,
        in_specs=specs,
        out_specs=tuple(VMEM for _ in outs),
        scratch_shapes=list(scratch),
        compiler_params=pltpu.CompilerParams(vmem_limit_bytes=limit * MIB),
        cost_estimate=cost,
        name=name,
    )(*ins)


def load_parts(source, target, sems, parts):
    rows = source.shape[0] // parts
    return [
        pltpu.make_async_copy(
            source.at[pl.ds(i * rows, rows)], target.at[pl.ds(i * rows, rows)], sems.at[i]
        )
        for i in range(parts)
    ]


LOADS = 4


def load_kernel(token_ref, *refs):
    count = (len(refs) - 2) // 2
    sources, targets = refs[:count], refs[count : 2 * count]
    done_ref, sems = refs[2 * count :]
    copies = []
    for i in range(count):
        copies += load_parts(sources[i], targets[i], sems.at[i], LOADS)
    for c in copies:
        c.start()
    done_ref[...] = token_ref[...]
    for c in copies:
        c.wait()


def load(token, *weights):
    return call(
        load_kernel,
        "load",
        tuple(pltpu.VMEM(w.shape, w.dtype) for w in weights) + (TOKEN,),
        (in_vmem(token),) + tuple(in_hbm(w) for w in weights),
        [VMEM] + [HBM] * len(weights),
        [pltpu.SemaphoreType.DMA((len(weights), LOADS))],
        limit=2,
        moved=sum(w.size * 2 for w in weights),
    )


def attend_kernel(
    lengths_hbm, q_hbm, cache_hbm, out_ref, lengths, queries, cache, sems, small_sems
):
    requests, width, length = cache.shape
    chunks = sems.shape[1]
    chunk = length // chunks
    devices, slots, latent = out_ref.shape
    heads = slots // requests
    scale = (HEAD_VALUE_WIDTH + ROTARY_WIDTH) ** (-0.5)

    def copy(r, c):
        at = pl.ds(c * chunk, chunk)
        return pltpu.make_async_copy(
            cache_hbm.at[r, :, at], cache.at[r, :, at], sems.at[r, c]
        )

    first = [
        pltpu.make_async_copy(lengths_hbm, lengths, small_sems.at[0]),
        pltpu.make_async_copy(q_hbm, queries, small_sems.at[1]),
    ]
    for c in first:
        c.start()
    for r in range(requests):
        for c in range(chunks):
            copy(r, c).start()
    for c in first:
        c.wait()
    results = []
    for r in range(requests):
        q = queries[r].astype(jnp.float32).T.astype(jnp.bfloat16)
        scores = []
        for c in range(chunks):
            copy(r, c).wait()
            s = jnp.dot(
                q,
                cache[r, :, c * chunk : (c + 1) * chunk],
                preferred_element_type=jnp.float32,
            )
            at = lax.broadcasted_iota(jnp.int32, s.shape, 1) + c * chunk
            scores.append(jnp.where(at < lengths[r], s * scale, -jnp.inf))
        scores = jnp.concatenate(scores, axis=1)
        peak = jnp.max(scores, axis=1, keepdims=True)
        e = jnp.exp(scores - peak)
        p = (e * (1.0 / jnp.sum(e, axis=1, keepdims=True))).astype(jnp.bfloat16)
        o = lax.dot_general(
            p,
            cache[r, :latent, :],
            (((1,), (1,)), ((), ())),
            preferred_element_type=jnp.float32,
        )
        results.append(o.reshape(devices, heads, latent))
    out_ref[...] = jnp.concatenate(results, axis=1).astype(out_ref.dtype)


def attend(queries, cache, lengths, devices):
    requests, heads, width = queries.shape
    length = cache.shape[1]
    slots = requests * heads // devices
    chunks = length // tile_of(length, 512)
    (out,) = call(
        attend_kernel,
        "attend",
        (jax.ShapeDtypeStruct((devices, slots, LATENT_WIDTH), jnp.bfloat16),),
        (
            in_hbm(lengths),
            in_hbm(jnp.swapaxes(queries, 1, 2)),
            in_hbm(jnp.swapaxes(cache, 1, 2)),
        ),
        [HBM] * 3,
        [
            pltpu.SMEM((requests,), jnp.int32),
            pltpu.VMEM((requests, width, heads), jnp.bfloat16),
            pltpu.VMEM((requests, width, length), jnp.bfloat16),
            pltpu.SemaphoreType.DMA((requests, chunks)),
            pltpu.SemaphoreType.DMA((2,)),
        ],
        limit=20,
    )
    return out


def relative(index, bits):
    out = jnp.zeros_like(index)
    for b in range(bits):
        out = out | (((index >> b) & 1) << (bits - 1 - b))
    return out


def row_order(me, rows, per, bits):
    i = lax.broadcasted_iota(jnp.int32, (rows, rows), 0)
    j = lax.broadcasted_iota(jnp.int32, (rows, rows), 1)
    shift = per.bit_length() - 1
    owner = relative(i >> shift, bits) ^ me
    return j == (owner << shift) + (i & (per - 1))


def column_copies(source, target, sems):
    tile = source.shape[1] // sems.shape[0]
    return [
        pltpu.make_async_copy(
            source.at[:, pl.ds(i * tile, tile)], target.at[:, pl.ds(i * tile, tile)], sems.at[i]
        )
        for i in range(sems.shape[0])
    ]


def project_kernel(bits, per, me_ref, latent_ref, up_ref, proj_hbm, keep_ref, send_ref, proj, sems):
    width = proj.shape[1]
    loads = column_copies(proj_hbm, proj, sems)
    tile = width // len(loads)
    for c in loads:
        c.start()
    heads, latent, value = up_ref.shape
    rows = latent_ref.shape[0] // heads
    half = rows // 2
    x = latent_ref[...]
    parts = []
    for h in range(heads):
        y = jnp.dot(x, up_ref[h], preferred_element_type=jnp.float32)
        y = y.reshape(rows, heads, value)
        mine = lax.broadcasted_iota(jnp.int32, y.shape, 1) == h
        parts.append(jnp.sum(jnp.where(mine, y, 0.0), axis=1))
    values = jnp.concatenate(parts, axis=1).astype(jnp.bfloat16)
    order = jnp.where(row_order(me_ref[0], rows, per, bits), 1.0, 0.0).astype(jnp.bfloat16)
    values = jnp.dot(order, values, preferred_element_type=jnp.float32).astype(jnp.bfloat16)
    for i, c in enumerate(loads):
        at = slice(i * tile, (i + 1) * tile)
        c.wait()
        y = jnp.dot(values, proj[:, at], preferred_element_type=jnp.float32)
        keep_ref[:, at] = y[:half]
        send_ref[:, at] = y[half:].astype(send_ref.dtype)


def project(me, latent, up, proj, per, bits):
    depth, width = proj.shape
    half = latent.shape[0] // up.shape[0] // 2
    return call(
        functools.partial(project_kernel, bits, per),
        "project",
        (pltpu.VMEM((half, width), jnp.float32), pltpu.VMEM((half, width), jnp.bfloat16)),
        (me, in_vmem(latent), in_vmem(up), in_hbm(proj)),
        [SMEM, VMEM, VMEM, HBM],
        [
            pltpu.VMEM(proj.shape, proj.dtype),
            pltpu.SemaphoreType.DMA((width // tile_of(width, 1024),)),
        ],
        limit=24,
    )


def fold_kernel(keep_ref, came_ref, token_ref, next_ref, send_ref, done_ref):
    half = next_ref.shape[0]
    total = keep_ref[...] + came_ref[...].astype(jnp.float32)
    next_ref[...] = total[:half]
    send_ref[...] = total[half:].astype(send_ref.dtype)
    done_ref[...] = token_ref[...]


def fold(keep, came, token):
    rows, width = keep.shape
    return call(
        fold_kernel,
        "fold",
        (
            pltpu.VMEM((rows // 2, width), jnp.float32),
            pltpu.VMEM((rows // 2, width), jnp.bfloat16),
            TOKEN,
        ),
        (in_vmem(keep), in_vmem(came), in_vmem(token)),
        [VMEM] * 3,
    )


def close_kernel(
    experts, keep_ref, came_ref, residual_ref, routes_ref, gates_ref, token_ref,
    total_ref, send_ref, done_ref,
):
    done_ref[...] = token_ref[...]
    per, width = residual_ref.shape
    total = keep_ref[...] + came_ref[...].astype(jnp.float32)
    own = total[:per] + residual_ref[...].astype(jnp.float32)
    total = jnp.concatenate([own, total[per:]], axis=0)
    lane = lax.broadcasted_iota(jnp.int32, (per, TABLE), 1)
    routes, gates = routes_ref[...], gates_ref[...]
    table = jnp.zeros((per, TABLE), jnp.float32)
    for t in range(routes.shape[1]):
        table += jnp.where(routes[:, t : t + 1] == lane % experts, gates[:, t : t + 1], 0.0)
    high = table.astype(jnp.bfloat16).astype(jnp.float32)
    middle = (table - high).astype(jnp.bfloat16).astype(jnp.float32)
    low = table - high - middle
    part = lane // experts
    table = jnp.where(
        part == 0, high, jnp.where(part == 1, middle, jnp.where(part == 2, low, 0.0))
    )
    table = jnp.concatenate([table, jnp.zeros_like(table)], axis=0)
    total_ref[:, :width] = total
    total_ref[:, width:] = table
    send_ref[:, :width] = total.astype(send_ref.dtype)
    send_ref[:, width:] = table.astype(send_ref.dtype)


def close(keep, came, residual, routes, gates, token, experts):
    rows, width = keep.shape
    shape = (rows, width + TABLE)
    return call(
        functools.partial(close_kernel, experts),
        "close",
        (pltpu.VMEM(shape, jnp.float32), pltpu.VMEM(shape, jnp.bfloat16), TOKEN),
        (in_vmem(keep), in_vmem(came), residual, routes, gates, in_vmem(token)),
        [VMEM] * 6,
    )


def norm_kernel(total_ref, came_ref, gain_ref, token_ref, attended_ref, normed_ref, done_ref):
    done_ref[...] = token_ref[...]
    per, width = attended_ref.shape
    came = came_ref[...].astype(jnp.float32)
    total = total_ref[...] + jnp.concatenate([came[per:], came[:per]], axis=0)
    attended = total[:, :width].astype(jnp.bfloat16).astype(jnp.float32)
    attended_ref[...] = attended[:per].astype(jnp.bfloat16)
    mean = jnp.mean(attended * attended, axis=1, keepdims=True)
    normed = attended * lax.rsqrt(mean + 1e-06) * gain_ref[...]
    normed_ref[:, :width] = normed.astype(jnp.bfloat16)
    normed_ref[:, width:] = total[:, width:].astype(jnp.bfloat16)


def norm(total, came, gain, token, per):
    rows, width = total.shape
    return call(
        norm_kernel,
        "norm",
        (
            pltpu.VMEM((per, width - TABLE), jnp.bfloat16),
            pltpu.VMEM((rows, width), jnp.bfloat16),
            TOKEN,
        ),
        (in_vmem(total), in_vmem(came), gain.reshape(1, -1), in_vmem(token)),
        [VMEM] * 4,
    )


def expert_kernel(blocks, experts, me_ref, *refs):
    gate, up, down_hbm, token_ref, keep_ref, send_ref, done_ref, down, sems = refs[blocks:]
    loads = column_copies(down_hbm, down, sems)
    for c in loads:
        c.start()
    done_ref[...] = token_ref[...]
    model, units = gate.shape
    tile = model // len(loads)
    half = keep_ref.shape[0]
    x = jnp.concatenate([r[...].astype(jnp.float32) for r in refs[:blocks]], axis=0)
    x = x.astype(jnp.bfloat16)
    table = x[:, model:].astype(jnp.float32)
    lane = lax.broadcasted_iota(jnp.int32, table.shape, 1)
    expert = (me_ref[0] * units) // FF_WIN
    mine = (lane % experts == expert) & (lane < 3 * experts)
    weight = jnp.sum(jnp.where(mine, table, 0.0), axis=1, keepdims=True)
    x = x[:, :model]
    g = jnp.dot(x, gate[...], preferred_element_type=jnp.float32)
    u = jnp.dot(x, up[...], preferred_element_type=jnp.float32)
    act = (g / (1.0 + jnp.exp(-g)) * u).astype(jnp.bfloat16)
    for i, c in enumerate(loads):
        at = slice(i * tile, (i + 1) * tile)
        c.wait()
        y = jnp.dot(act, down[:, at], preferred_element_type=jnp.float32) * weight
        keep_ref[:, at] = y[:half]
        send_ref[:, at] = y[half:].astype(send_ref.dtype)


def expert(me, blocks, gate, up, down, token, experts):
    model, units = gate.shape
    half = sum(b.shape[0] for b in blocks) // 2
    return call(
        functools.partial(expert_kernel, len(blocks), experts),
        "expert",
        (
            pltpu.VMEM((half, model), jnp.float32),
            pltpu.VMEM((half, model), jnp.bfloat16),
            TOKEN,
        ),
        (me,)
        + tuple(in_vmem(b) for b in blocks)
        + (in_vmem(gate), in_vmem(up), in_hbm(down), in_vmem(token)),
        [SMEM] + [VMEM] * (len(blocks) + 2) + [HBM, VMEM],
        [
            pltpu.VMEM(down.shape, down.dtype),
            pltpu.SemaphoreType.DMA((model // tile_of(model, 1024),)),
        ],
        limit=24,
    )


def last_kernel(keep_ref, came_ref, out_ref):
    out_ref[...] = (keep_ref[...] + came_ref[...].astype(jnp.float32)).astype(out_ref.dtype)


def body(
    queries,
    latent_key_cache,
    lengths,
    value_up_weight,
    out_proj,
    residual_in,
    norm_gain,
    w_gate,
    w_up,
    w_down,
    routes,
    route_gates,
):
    devices = lax.axis_size("exp")
    bits = devices.bit_length() - 1
    per = queries.shape[0]
    experts = devices * w_gate.shape[1] // FF_WIN
    me = lax.axis_index("exp").astype(jnp.int32).reshape(1)

    def swap(x, bit):
        return lax.ppermute(x, "exp", [(i, i ^ (1 << bit)) for i in range(devices)])

    latent = attend(queries, latent_key_cache, lengths, devices)
    latent = lax.all_to_all(latent, "exp", split_axis=0, concat_axis=0, tiled=True)
    latent = latent.reshape(-1, LATENT_WIDTH)
    keep, send = project(me, latent, value_up_weight, out_proj, per, bits)
    token = jnp.zeros(TOKEN.shape, TOKEN.dtype)
    for bit in range(bits - 2):
        came = swap(send, bit)
        if bit == 1:
            gate, token = load(token, w_gate)
        keep, send, token = fold(keep, came, token)
    came = swap(send, bits - 2)
    total, send, token = close(keep, came, residual_in, routes, route_gates, token, experts)
    came = swap(send, bits - 1)
    up, token = load(token, w_up)
    attended, x, token = norm(total, came, norm_gain, token, per)
    blocks = [x]
    for bit in reversed(range(bits - 1)):
        if bit > 2:
            blocks = [jnp.concatenate(blocks + [swap(b, bit) for b in blocks], axis=0)]
        else:
            blocks = blocks + [swap(b, bit) for b in blocks]
    keep, send, token = expert(me, blocks, gate, up, w_down, token, experts)
    for bit in range(bits - 1):
        keep, send, token = fold(keep, swap(send, bit), token)
    (mixed,) = call(
        last_kernel,
        "last",
        (jax.ShapeDtypeStruct(attended.shape, jnp.bfloat16),),
        (in_vmem(keep), in_vmem(swap(send, bits - 1))),
        [VMEM] * 2,
    )
    return attended, mixed


def solution(mesh):
    placed = (
        P(("grp", "exp"), None, None),
        P(("grp", "exp"), None, None),
        P(("grp", "exp")),
        P("exp", None, None),
        P("exp", None),
        P(("grp", "exp"), None),
        P(),
        P(None, "exp"),
        P(None, "exp"),
        P("exp", None),
        P(("grp", "exp"), None),
        P(("grp", "exp"), None),
    )
    return jax.shard_map(
        body,
        mesh=mesh,
        in_specs=placed,
        out_specs=(P(("grp", "exp"), None), P(("grp", "exp"), None)),
        check_vma=False,
    )
```

```python
import functools

import jax
import jax.numpy as jnp
from jax import lax
from jax.experimental import pallas as pl
from jax.experimental.pallas import tpu as pltpu
from jax.sharding import PartitionSpec as P

LATENT_WIDTH = 512
ROTARY_WIDTH = 64
HEAD_VALUE_WIDTH = 128
FF_WIN = 1024
TABLE = 128
MIB = 1 << 20

HBM = pl.BlockSpec(memory_space=pl.ANY)
VMEM = pl.BlockSpec(memory_space=pltpu.VMEM)
SMEM = pl.BlockSpec(memory_space=pltpu.SMEM)


def tile_of(extent, wanted):
    while extent % wanted:
        wanted //= 2
    return wanted


def in_hbm(x):
    return pltpu.with_memory_space_constraint(x, pltpu.HBM)


def in_vmem(x):
    return pltpu.with_memory_space_constraint(x, pltpu.VMEM)


TOKEN = pltpu.VMEM((8, 128), jnp.float32)


def call(kernel, name, outs, ins, specs, scratch=(), limit=4, moved=None):
    cost = None
    if moved:
        cost = pl.CostEstimate(flops=0, bytes_accessed=moved, transcendentals=0)
    return pl.pallas_call(
        kernel,
        out_shape=outs,
        in_specs=specs,
        out_specs=tuple(VMEM for _ in outs),
        scratch_shapes=list(scratch),
        compiler_params=pltpu.CompilerParams(vmem_limit_bytes=limit * MIB),
        cost_estimate=cost,
        name=name,
    )(*ins)


def row_copy(source, target, sems, i):
    rows = source.shape[0] // sems.shape[0]
    at = pl.ds(pl.multiple_of(i * rows, rows), rows)
    return pltpu.make_async_copy(source.at[at], target.at[at], sems.at[i])


def column_copy(source, target, sems, i):
    tile = source.shape[1] // sems.shape[0]
    at = pl.ds(pl.multiple_of(i * tile, tile), tile)
    return pltpu.make_async_copy(source.at[:, at], target.at[:, at], sems.at[i])


def start_all(count, copy):
    def step(i, carry):
        copy(i).start()
        return carry

    lax.fori_loop(0, count, step, 0)


LOADS = 4


def load_kernel(token_ref, *refs):
    count = (len(refs) - 2) // 2
    sources, targets = refs[:count], refs[count : 2 * count]
    done_ref, sems = refs[2 * count :]
    copies = [
        row_copy(sources[i], targets[i], sems.at[i], part)
        for i in range(count)
        for part in range(LOADS)
    ]
    for c in copies:
        c.start()
    done_ref[...] = token_ref[...]
    for c in copies:
        c.wait()


def load(token, *weights):
    return call(
        load_kernel,
        "load",
        tuple(pltpu.VMEM(w.shape, w.dtype) for w in weights) + (TOKEN,),
        (in_vmem(token),) + tuple(in_hbm(w) for w in weights),
        [VMEM] + [HBM] * len(weights),
        [pltpu.SemaphoreType.DMA((len(weights), LOADS))],
        limit=2,
        moved=sum(w.size * 2 for w in weights),
    )


def attend_kernel(
    me_ref, lengths_hbm, q_hbm, cache_hbm, proj_hbm, out_ref, proj,
    lengths, queries, cache, sems, small_sems, proj_sems,
):
    requests, width, length = cache.shape
    chunks = sems.shape[1]
    chunk = length // chunks
    devices, slots, latent = out_ref.shape
    heads = slots // requests
    scale = (HEAD_VALUE_WIDTH + ROTARY_WIDTH) ** (-0.5)
    load = functools.partial(
        row_copy, proj_hbm.at[:, pl.ds(0, proj.shape[1])], proj, proj_sems
    )

    def copy(r, c):
        at = pl.ds(pl.multiple_of(c * chunk, chunk), chunk)
        return pltpu.make_async_copy(
            cache_hbm.at[r, :, at], cache.at[r, :, at], sems.at[r, c]
        )

    first = [
        pltpu.make_async_copy(lengths_hbm, lengths, small_sems.at[0]),
        pltpu.make_async_copy(q_hbm, queries, small_sems.at[1]),
    ]
    for c in first:
        c.start()
    for r in range(requests):
        start_all(chunks, functools.partial(copy, r))
    for c in first:
        c.wait()
    scores = []
    for r in range(requests):
        q = queries[r].astype(jnp.float32).T.astype(jnp.bfloat16)
        parts = []
        for c in range(chunks):
            copy(r, c).wait()
            s = jnp.dot(
                q,
                cache[r, :, c * chunk : (c + 1) * chunk],
                preferred_element_type=jnp.float32,
            )
            at = lax.broadcasted_iota(jnp.int32, s.shape, 1) + c * chunk
            parts.append(jnp.where(at < lengths[r], s * scale, -jnp.inf))
        scores.append(jnp.concatenate(parts, axis=1))
        if r == 0:
            start_all(LOADS, load)
    results = []
    for r in range(requests):
        peak = jnp.max(scores[r], axis=1, keepdims=True)
        e = jnp.exp(scores[r] - peak)
        p = (e * (1.0 / jnp.sum(e, axis=1, keepdims=True))).astype(jnp.bfloat16)
        o = lax.dot_general(
            p,
            cache[r, :latent, :],
            (((1,), (1,)), ((), ())),
            preferred_element_type=jnp.float32,
        )
        results.append(o.reshape(devices, heads, latent))
    out_ref[...] = jnp.concatenate(results, axis=1).astype(out_ref.dtype)
    for i in range(LOADS):
        load(i).wait()


def attend(me, queries, cache, lengths, proj, early, devices):
    requests, heads, width = queries.shape
    length = cache.shape[1]
    slots = requests * heads // devices
    chunks = length // tile_of(length, 1024)
    return call(
        attend_kernel,
        "attend",
        (
            pltpu.VMEM((devices, slots, LATENT_WIDTH), jnp.bfloat16),
            pltpu.VMEM((proj.shape[0], early), proj.dtype),
        ),
        (
            me,
            in_hbm(lengths),
            in_hbm(jnp.swapaxes(queries, 1, 2)),
            in_hbm(jnp.swapaxes(cache, 1, 2)),
            in_hbm(proj),
        ),
        [SMEM] + [HBM] * 4,
        [
            pltpu.SMEM((requests,), jnp.int32),
            pltpu.VMEM((requests, width, heads), jnp.bfloat16),
            pltpu.VMEM((requests, width, length), jnp.bfloat16),
            pltpu.SemaphoreType.DMA((requests, chunks)),
            pltpu.SemaphoreType.DMA((2,)),
            pltpu.SemaphoreType.DMA((LOADS,)),
        ],
        limit=20,
    )


def relative(index, bits):
    out = jnp.zeros_like(index)
    for b in range(bits):
        out = out | (((index >> b) & 1) << (bits - 1 - b))
    return out


def row_order(me, rows, per, bits):
    i = lax.broadcasted_iota(jnp.int32, (rows, rows), 0)
    j = lax.broadcasted_iota(jnp.int32, (rows, rows), 1)
    shift = per.bit_length() - 1
    owner = relative(i >> shift, bits) ^ me
    return j == (owner << shift) + (i & (per - 1))


def project_kernel(
    bits, per, me_ref, latent_ref, up_ref, proj_hbm, first, keep_ref, send_ref, rest, sems
):
    tile = rest.shape[1] // sems.shape[0]
    early = first.shape[1]
    source = proj_hbm.at[:, pl.ds(early, rest.shape[1])]
    load = functools.partial(column_copy, source, rest, sems)
    start_all(sems.shape[0], load)
    heads, latent, value = up_ref.shape
    rows = latent_ref.shape[0] // heads
    half = rows // 2
    x = latent_ref[...]
    parts = []
    for h in range(heads):
        y = jnp.dot(x, up_ref[h], preferred_element_type=jnp.float32)
        y = y.reshape(rows, heads, value)
        mine = lax.broadcasted_iota(jnp.int32, y.shape, 1) == h
        parts.append(jnp.sum(jnp.where(mine, y, 0.0), axis=1))
    values = jnp.concatenate(parts, axis=1).astype(jnp.bfloat16)
    order = jnp.where(row_order(me_ref[0], rows, per, bits), 1.0, 0.0).astype(jnp.bfloat16)
    values = jnp.dot(order, values, preferred_element_type=jnp.float32).astype(jnp.bfloat16)

    def multiply(weights, at, to):
        y = jnp.dot(values, weights[:, at : at + tile], preferred_element_type=jnp.float32)
        keep_ref[:, to : to + tile] = y[:half]
        send_ref[:, to : to + tile] = y[half:].astype(send_ref.dtype)

    for t in range(0, early, tile):
        multiply(first, t, t)
    for i in range(sems.shape[0]):
        load(i).wait()
        multiply(rest, i * tile, early + i * tile)


def project(me, latent, up, proj, first, per, bits):
    depth, width = proj.shape
    late = width - first.shape[1]
    half = latent.shape[0] // up.shape[0] // 2
    return call(
        functools.partial(project_kernel, bits, per),
        "project",
        (pltpu.VMEM((half, width), jnp.float32), pltpu.VMEM((half, width), jnp.bfloat16)),
        (me, in_vmem(latent), in_vmem(up), in_hbm(proj), in_vmem(first)),
        [SMEM, VMEM, VMEM, HBM, VMEM],
        [
            pltpu.VMEM((depth, late), proj.dtype),
            pltpu.SemaphoreType.DMA((late // tile_of(late, 512),)),
        ],
        limit=14,
        moved=100 * MIB,
    )


def fold_kernel(parts, keep_ref, came_ref, *refs):
    rows = keep_ref.shape[0] // parts
    outs = refs[len(refs) - parts - 1 :]
    total = keep_ref[...] + came_ref[...].astype(jnp.float32)
    outs[0][...] = total[:rows]
    for i in range(1, parts):
        outs[i][...] = total[i * rows : (i + 1) * rows].astype(outs[i].dtype)
    outs[parts][...] = refs[0][...]


def fold(keep, came, token, parts=2):
    rows, width = keep.shape
    return call(
        functools.partial(fold_kernel, parts),
        "fold",
        (pltpu.VMEM((rows // parts, width), jnp.float32),)
        + (pltpu.VMEM((rows // parts, width), jnp.bfloat16),) * (parts - 1)
        + (TOKEN,),
        (in_vmem(keep), in_vmem(came), in_vmem(token)),
        [VMEM] * 3,
    )


def gather_kernel(keep_ref, first_ref, second_ref, third_ref, token_ref, next_ref, send_ref, done_ref):
    half = next_ref.shape[0]
    total = keep_ref[...] + first_ref[...].astype(jnp.float32)
    total += second_ref[...].astype(jnp.float32) + third_ref[...].astype(jnp.float32)
    next_ref[...] = total[:half]
    send_ref[...] = total[half:].astype(send_ref.dtype)
    done_ref[...] = token_ref[...]


def gather(keep, came, token):
    rows, width = keep.shape
    return call(
        gather_kernel,
        "gather",
        (
            pltpu.VMEM((rows // 2, width), jnp.float32),
            pltpu.VMEM((rows // 2, width), jnp.bfloat16),
            TOKEN,
        ),
        (in_vmem(keep),) + tuple(in_vmem(c) for c in came) + (in_vmem(token),),
        [VMEM] * 5,
    )


def close_kernel(
    experts, keep_ref, first_ref, second_ref, third_ref, residual_ref, routes_ref, gates_ref,
    token_ref, total_ref, send_ref, done_ref,
):
    done_ref[...] = token_ref[...]
    per, width = residual_ref.shape
    total = keep_ref[...] + first_ref[...].astype(jnp.float32)
    total += second_ref[...].astype(jnp.float32) + third_ref[...].astype(jnp.float32)
    own = total[:per] + residual_ref[...].astype(jnp.float32)
    total = jnp.concatenate([own, total[per:]], axis=0)
    lane = lax.broadcasted_iota(jnp.int32, (per, TABLE), 1)
    routes, gates = routes_ref[...], gates_ref[...]
    table = jnp.zeros((per, TABLE), jnp.float32)
    for t in range(routes.shape[1]):
        table += jnp.where(routes[:, t : t + 1] == lane % experts, gates[:, t : t + 1], 0.0)
    high = table.astype(jnp.bfloat16).astype(jnp.float32)
    middle = (table - high).astype(jnp.bfloat16).astype(jnp.float32)
    low = table - high - middle
    part = lane // experts
    table = jnp.where(
        part == 0, high, jnp.where(part == 1, middle, jnp.where(part == 2, low, 0.0))
    )
    table = jnp.concatenate([table, jnp.zeros_like(table)], axis=0)
    total_ref[:, :width] = total
    total_ref[:, width:] = table
    send_ref[:, :width] = total.astype(send_ref.dtype)
    send_ref[:, width:] = table.astype(send_ref.dtype)


def close(keep, came, residual, routes, gates, token, experts):
    rows, width = keep.shape
    shape = (rows, width + TABLE)
    return call(
        functools.partial(close_kernel, experts),
        "close",
        (pltpu.VMEM(shape, jnp.float32), pltpu.VMEM(shape, jnp.bfloat16), TOKEN),
        (in_vmem(keep),)
        + tuple(in_vmem(c) for c in came)
        + (residual, routes, gates, in_vmem(token)),
        [VMEM] * 8,
    )


def norm_kernel(total_ref, came_ref, gain_ref, token_ref, attended_ref, normed_ref, done_ref):
    done_ref[...] = token_ref[...]
    per, width = attended_ref.shape
    came = came_ref[...].astype(jnp.float32)
    total = total_ref[...] + jnp.concatenate([came[per:], came[:per]], axis=0)
    attended = total[:, :width].astype(jnp.bfloat16).astype(jnp.float32)
    attended_ref[...] = attended[:per].astype(jnp.bfloat16)
    mean = jnp.mean(attended * attended, axis=1, keepdims=True)
    normed = attended * lax.rsqrt(mean + 1e-06) * gain_ref[...]
    normed_ref[:, :width] = normed.astype(jnp.bfloat16)
    normed_ref[:, width:] = total[:, width:].astype(jnp.bfloat16)


def norm(total, came, gain, token, per):
    rows, width = total.shape
    return call(
        norm_kernel,
        "norm",
        (
            pltpu.VMEM((per, width - TABLE), jnp.bfloat16),
            pltpu.VMEM((rows, width), jnp.bfloat16),
            TOKEN,
        ),
        (in_vmem(total), in_vmem(came), gain.reshape(1, -1), in_vmem(token)),
        [VMEM] * 4,
    )


def expert_kernel(blocks, experts, me_ref, *refs):
    gate, up, down_hbm, token_ref, keep_ref, send_ref, done_ref, down, sems = refs[blocks:]
    start_all(sems.shape[0], functools.partial(column_copy, down_hbm, down, sems))
    done_ref[...] = token_ref[...]
    model, units = gate.shape
    tile = model // sems.shape[0]
    half = keep_ref.shape[0]
    x = jnp.concatenate([r[...].astype(jnp.float32) for r in refs[:blocks]], axis=0)
    x = x.astype(jnp.bfloat16)
    table = x[:, model:].astype(jnp.float32)
    lane = lax.broadcasted_iota(jnp.int32, table.shape, 1)
    expert = (me_ref[0] * units) // FF_WIN
    mine = (lane % experts == expert) & (lane < 3 * experts)
    weight = jnp.sum(jnp.where(mine, table, 0.0), axis=1, keepdims=True)
    x = x[:, :model]
    g = jnp.dot(x, gate[...], preferred_element_type=jnp.float32)
    u = jnp.dot(x, up[...], preferred_element_type=jnp.float32)
    act = (g / (1.0 + jnp.exp(-g)) * u).astype(jnp.bfloat16)
    for i in range(sems.shape[0]):
        at = slice(i * tile, (i + 1) * tile)
        column_copy(down_hbm, down, sems, i).wait()
        y = jnp.dot(act, down[:, at], preferred_element_type=jnp.float32) * weight
        keep_ref[:, at] = y[:half]
        send_ref[:, at] = y[half:].astype(send_ref.dtype)


def expert(me, blocks, gate, up, down, token, experts):
    model, units = gate.shape
    half = sum(b.shape[0] for b in blocks) // 2
    return call(
        functools.partial(expert_kernel, len(blocks), experts),
        "expert",
        (
            pltpu.VMEM((half, model), jnp.float32),
            pltpu.VMEM((half, model), jnp.bfloat16),
            TOKEN,
        ),
        (me,)
        + tuple(in_vmem(b) for b in blocks)
        + (in_vmem(gate), in_vmem(up), in_hbm(down), in_vmem(token)),
        [SMEM] + [VMEM] * (len(blocks) + 2) + [HBM, VMEM],
        [
            pltpu.VMEM(down.shape, down.dtype),
            pltpu.SemaphoreType.DMA((model // tile_of(model, 1024),)),
        ],
        limit=24,
    )


def last_kernel(keep_ref, came_ref, token_ref, out_ref):
    out_ref[...] = (keep_ref[...] + came_ref[...].astype(jnp.float32)).astype(out_ref.dtype)


def body(
    queries,
    latent_key_cache,
    lengths,
    value_up_weight,
    out_proj,
    residual_in,
    norm_gain,
    w_gate,
    w_up,
    w_down,
    routes,
    route_gates,
):
    devices = lax.axis_size("exp")
    bits = devices.bit_length() - 1
    per = queries.shape[0]
    experts = devices * w_gate.shape[1] // FF_WIN
    me = lax.axis_index("exp").astype(jnp.int32).reshape(1)

    def swap(x, *some_bits):
        mask = sum(1 << bit for bit in some_bits)
        return lax.ppermute(x, "exp", [(i, i ^ mask) for i in range(devices)])

    def square(sends):
        low, high = bits - 3, bits - 2
        return swap(sends[0], high), swap(sends[1], low), swap(sends[2], low, high)

    early = out_proj.shape[1] // 2
    latent, first = attend(me, queries, latent_key_cache, lengths, out_proj, early, devices)
    latent = lax.all_to_all(latent, "exp", split_axis=0, concat_axis=0, tiled=True)
    latent = latent.reshape(-1, LATENT_WIDTH)
    keep, send = project(me, latent, value_up_weight, out_proj, first, per, bits)
    token = jnp.zeros(TOKEN.shape, TOKEN.dtype)
    for bit in range(bits - 4):
        keep, send, token = fold(keep, swap(send, bit), token)
    keep, *sends, token = fold(keep, swap(send, bits - 4), token, 4)
    came = square(sends)
    total, send, token = close(keep, came, residual_in, routes, route_gates, token, experts)
    came = swap(send, bits - 1)
    attended, x, token = norm(total, came, norm_gain, token, per)
    for bit in reversed(range(bits - 1)):
        if bit > 2:
            x = jnp.concatenate([x, swap(x, bit)], axis=0)
        elif bit == 2:
            blocks = [x, swap(x, 2), swap(x, 1), swap(x, 2, 1)]
        elif bit == 0:
            blocks = blocks + [swap(b, 0) for b in blocks]
    keep, send, token = expert(me, blocks, w_gate, w_up, w_down, token, experts)
    for bit in range(bits - 4):
        keep, send, token = fold(keep, swap(send, bit), token)
    keep, *sends, token = fold(keep, swap(send, bits - 4), token, 4)
    keep, send, token = gather(keep, square(sends), token)
    (mixed,) = call(
        last_kernel,
        "last",
        (jax.ShapeDtypeStruct(attended.shape, jnp.bfloat16),),
        (in_vmem(keep), in_vmem(swap(send, bits - 1)), in_vmem(token)),
        [VMEM] * 3,
    )
    return attended, mixed


def solution(mesh):
    placed = (
        P(("grp", "exp"), None, None),
        P(("grp", "exp"), None, None),
        P(("grp", "exp")),
        P("exp", None, None),
        P("exp", None),
        P(("grp", "exp"), None),
        P(),
        P(None, "exp"),
        P(None, "exp"),
        P("exp", None),
        P(("grp", "exp"), None),
        P(("grp", "exp"), None),
    )
    return jax.shard_map(
        body,
        mesh=mesh,
        in_specs=placed,
        out_specs=(P(("grp", "exp"), None), P(("grp", "exp"), None)),
        check_vma=False,
    )
```

```python
import functools

import jax
import jax.numpy as jnp
from jax import lax
from jax.experimental import pallas as pl
from jax.experimental.pallas import tpu as pltpu
from jax.sharding import PartitionSpec as P

LATENT_WIDTH = 512
ROTARY_WIDTH = 64
HEAD_VALUE_WIDTH = 128
FF_WIN = 1024
TABLE = 128
MIB = 1 << 20

HBM = pl.BlockSpec(memory_space=pl.ANY)
VMEM = pl.BlockSpec(memory_space=pltpu.VMEM)
SMEM = pl.BlockSpec(memory_space=pltpu.SMEM)


def tile_of(extent, wanted):
    while extent % wanted:
        wanted //= 2
    return wanted


def in_hbm(x):
    return pltpu.with_memory_space_constraint(x, pltpu.HBM)


def in_vmem(x):
    return pltpu.with_memory_space_constraint(x, pltpu.VMEM)


TOKEN = pltpu.VMEM((8, 128), jnp.float32)


def tall(x):
    rows = x.shape[0]
    if rows >= 128:
        return x
    return jnp.concatenate([x, jnp.zeros((128 - rows, x.shape[1]), x.dtype)], axis=0)


def call(kernel, name, outs, ins, specs, scratch=(), limit=4, moved=None):
    cost = None
    if moved:
        cost = pl.CostEstimate(flops=0, bytes_accessed=moved, transcendentals=0)
    return pl.pallas_call(
        kernel,
        out_shape=outs,
        in_specs=specs,
        out_specs=tuple(VMEM for _ in outs),
        scratch_shapes=list(scratch),
        compiler_params=pltpu.CompilerParams(vmem_limit_bytes=limit * MIB),
        cost_estimate=cost,
        name=name,
    )(*ins)


def row_copy(source, target, sems, i):
    rows = source.shape[0] // sems.shape[0]
    at = pl.ds(pl.multiple_of(i * rows, rows), rows)
    return pltpu.make_async_copy(source.at[at], target.at[at], sems.at[i])


def column_copy(source, target, sems, i):
    tile = source.shape[1] // sems.shape[0]
    at = pl.ds(pl.multiple_of(i * tile, tile), tile)
    return pltpu.make_async_copy(source.at[:, at], target.at[:, at], sems.at[i])


def start_all(count, copy):
    def step(i, carry):
        copy(i).start()
        return carry

    lax.fori_loop(0, count, step, 0)


LOADS = 4


def load_kernel(token_ref, source, target, done_ref, sems):
    source = source.at[:, pl.ds(0, target.shape[1])]
    copies = [row_copy(source, target, sems, part) for part in range(LOADS)]
    for c in copies:
        c.start()
    done_ref[...] = token_ref[...]
    for c in copies:
        c.wait()


def load(token, weight, columns):
    return call(
        load_kernel,
        "load",
        (pltpu.VMEM((weight.shape[0], columns), weight.dtype), TOKEN),
        (in_vmem(token), in_hbm(weight)),
        [VMEM, HBM],
        [pltpu.SemaphoreType.DMA((LOADS,))],
        limit=2,
        moved=weight.shape[0] * columns * 2,
    )


def attend_kernel(
    bits, me_ref, lengths_hbm, q_hbm, cache_hbm, *refs
):
    outs = refs[:-5]
    lengths, queries, cache, sems, small_sems = refs[-5:]
    requests, width, length = cache.shape
    chunks = sems.shape[1]
    chunk = length // chunks
    latent = outs[0].shape[-1]
    heads = queries.shape[2]
    here = heads >> bits
    scale = (HEAD_VALUE_WIDTH + ROTARY_WIDTH) ** (-0.5)

    def copy(r, c):
        at = pl.ds(pl.multiple_of(c * chunk, chunk), chunk)
        return pltpu.make_async_copy(
            cache_hbm.at[r, :, at], cache.at[r, :, at], sems.at[r, c]
        )

    first = [
        pltpu.make_async_copy(lengths_hbm, lengths, small_sems.at[0]),
        pltpu.make_async_copy(q_hbm, queries, small_sems.at[1]),
    ]
    for c in first:
        c.start()
    for r in range(requests):
        start_all(chunks, functools.partial(copy, r))
    for c in first:
        c.wait()
    at = me_ref[0] if len(outs) == 2 else None
    order = one_hot(row_order(at, heads, here, bits))
    scores = []
    for r in range(requests):
        q = lax.dot_general(
            order,
            queries[r],
            (((1,), (1,)), ((), ())),
            preferred_element_type=jnp.float32,
        ).astype(jnp.bfloat16)
        parts = []
        for c in range(chunks):
            copy(r, c).wait()
            s = jnp.dot(
                q,
                cache[r, :, c * chunk : (c + 1) * chunk],
                preferred_element_type=jnp.float32,
            )
            at = lax.broadcasted_iota(jnp.int32, s.shape, 1) + c * chunk
            parts.append(jnp.where(at < lengths[r], s * scale, -jnp.inf))
        scores.append(jnp.concatenate(parts, axis=1))
    results = []
    for r in range(requests):
        peak = jnp.max(scores[r], axis=1, keepdims=True)
        e = jnp.exp(scores[r] - peak)
        p = (e * (1.0 / jnp.sum(e, axis=1, keepdims=True))).astype(jnp.bfloat16)
        o = lax.dot_general(
            p,
            cache[r, :latent, :],
            (((1,), (1,)), ((), ())),
            preferred_element_type=jnp.float32,
        )
        results.append(o.reshape(1 << bits, here, latent))
    out = jnp.concatenate(results, axis=1).astype(jnp.bfloat16)
    share = (1 << bits) // len(outs)
    for i, ref in enumerate(outs):
        ref[...] = out[i * share : (i + 1) * share]


def attend(me, queries, cache, lengths, bits, sides):
    requests, heads, width = queries.shape
    length = cache.shape[1]
    devices = 1 << bits
    slots = requests * heads // devices
    chunks = length // tile_of(length, 1024)
    return call(
        functools.partial(attend_kernel, bits),
        "attend",
        (pltpu.VMEM((devices // sides, slots, LATENT_WIDTH), jnp.bfloat16),) * sides,
        (
            me,
            in_hbm(lengths),
            in_hbm(jnp.swapaxes(queries, 1, 2)),
            in_hbm(jnp.swapaxes(cache, 1, 2)),
        ),
        [SMEM] + [HBM] * 3,
        [
            pltpu.SMEM((requests,), jnp.int32),
            pltpu.VMEM((requests, width, heads), jnp.bfloat16),
            pltpu.VMEM((requests, width, length), jnp.bfloat16),
            pltpu.SemaphoreType.DMA((requests, chunks)),
            pltpu.SemaphoreType.DMA((2,)),
        ],
        limit=16,
    )


def pack_kernel(own_ref, came_ref, token_ref, *refs):
    *outs, done_ref = refs
    for i, ref in enumerate(outs):
        for far in range(2):
            ref[far, 0] = own_ref[2 * i + far]
            ref[far, 1] = came_ref[2 * i + far]
    done_ref[...] = token_ref[...]


def pack(own, came, token):
    shape = (2, 2) + own.shape[1:]
    return call(
        pack_kernel,
        "pack",
        (pltpu.VMEM(shape, own.dtype),) * 4 + (TOKEN,),
        (in_vmem(own), in_vmem(came), in_vmem(token)),
        [VMEM] * 3,
    )


def split_kernel(*refs):
    *sources, token_ref, keep_ref, send_ref, done_ref = refs
    for i, ref in enumerate(sources):
        keep_ref[i] = ref[0]
        send_ref[i] = ref[1]
    done_ref[...] = token_ref[...]


def split(blocks, token):
    shape = (len(blocks),) + blocks[0].shape[1:]
    return call(
        split_kernel,
        "split",
        (pltpu.VMEM(shape, blocks[0].dtype),) * 2 + (TOKEN,),
        tuple(in_vmem(b) for b in blocks) + (in_vmem(token),),
        [VMEM] * (len(blocks) + 1),
    )


def relative(index, bits):
    out = jnp.zeros_like(index)
    for b in range(bits):
        out = out | (((index >> b) & 1) << (bits - 1 - b))
    return out


def row_order(me, rows, per, bits):
    i = lax.broadcasted_iota(jnp.int32, (rows, rows), 0)
    j = lax.broadcasted_iota(jnp.int32, (rows, rows), 1)
    if me is None:
        return i == j
    shift = per.bit_length() - 1
    owner = relative(i >> shift, bits) ^ me
    return j == (owner << shift) + (i & (per - 1))


def square_order(rows, per):
    i = lax.broadcasted_iota(jnp.int32, (rows, rows), 0)
    j = lax.broadcasted_iota(jnp.int32, (rows, rows), 1)
    shift = per.bit_length() - 1
    q = i >> shift
    owner = ((q & 1) << 3) | (q & 6) | (q >> 3)
    return j == (owner << shift) + (i & (per - 1))


def one_hot(order):
    return jnp.where(order, 1.0, 0.0).astype(jnp.bfloat16)


def project_kernel(
    bits, per, me_ref, up_ref, proj_hbm, first, *refs
):
    *latents, keep_ref, send_ref, rest, sems = refs
    tile = rest.shape[1] // sems.shape[0]
    early = first.shape[1]
    source = proj_hbm.at[:, pl.ds(early, rest.shape[1])]
    load = functools.partial(column_copy, source, rest, sems)
    start_all(sems.shape[0], load)
    heads, latent, value = up_ref.shape
    x = jnp.concatenate([ref[...] for ref in latents], axis=0)
    rows = x.shape[0] // heads
    half = rows // 2
    parts = []
    together = min(2, heads)
    for h in range(0, heads, together):
        up = jnp.concatenate([up_ref[h + i] for i in range(together)], axis=1)
        y = jnp.dot(x, up, preferred_element_type=jnp.float32)
        y = y.reshape(rows, heads, together * value)
        head = lax.broadcasted_iota(jnp.int32, y.shape, 1)
        lane = lax.broadcasted_iota(jnp.int32, y.shape, 2)
        parts.append(jnp.sum(jnp.where(head == h + lane // value, y, 0.0), axis=1))
    values = jnp.concatenate(parts, axis=1).astype(jnp.bfloat16)
    if len(latents) == 2:
        order = square_order(rows, per)
    else:
        order = row_order(me_ref[0], rows, per, bits)
    values = jnp.dot(one_hot(order), values, preferred_element_type=jnp.float32).astype(jnp.bfloat16)
    values = tall(values)

    def multiply(weights, at, to):
        y = jnp.dot(values, weights[:, at : at + tile], preferred_element_type=jnp.float32)
        keep_ref[:, to : to + tile] = y[:half]
        send_ref[:, to : to + tile] = y[half:rows].astype(send_ref.dtype)

    for t in range(0, early, tile):
        multiply(first, t, t)
    for i in range(sems.shape[0]):
        load(i).wait()
        multiply(rest, i * tile, early + i * tile)


def project(me, latents, up, proj, first, per, bits):
    depth, width = proj.shape
    late = width - first.shape[1]
    half = sum(x.shape[0] for x in latents) // up.shape[0] // 2
    return call(
        functools.partial(project_kernel, bits, per),
        "project",
        (pltpu.VMEM((half, width), jnp.float32), pltpu.VMEM((half, width), jnp.bfloat16)),
        (me, in_vmem(up), in_hbm(proj), in_vmem(first)) + tuple(in_vmem(x) for x in latents),
        [SMEM, VMEM, HBM, VMEM] + [VMEM] * len(latents),
        [
            pltpu.VMEM((depth, late), proj.dtype),
            pltpu.SemaphoreType.DMA((late // tile_of(late, 512),)),
        ],
        limit=6,
        moved=100 * MIB,
    )


def fold_kernel(parts, keep_ref, came_ref, *refs):
    rows = keep_ref.shape[0] // parts
    outs = refs[len(refs) - parts - 1 :]
    total = keep_ref[...] + came_ref[...].astype(jnp.float32)
    outs[0][...] = total[:rows]
    for i in range(1, parts):
        outs[i][...] = total[i * rows : (i + 1) * rows].astype(outs[i].dtype)
    outs[parts][...] = refs[0][...]


def fold(keep, came, token, parts=2):
    rows, width = keep.shape
    return call(
        functools.partial(fold_kernel, parts),
        "fold",
        (pltpu.VMEM((rows // parts, width), jnp.float32),)
        + (pltpu.VMEM((rows // parts, width), jnp.bfloat16),) * (parts - 1)
        + (TOKEN,),
        (in_vmem(keep), in_vmem(came), in_vmem(token)),
        [VMEM] * 3,
    )


def gather_kernel(keep_ref, first_ref, second_ref, third_ref, token_ref, next_ref, send_ref, done_ref):
    half = next_ref.shape[0]
    total = keep_ref[...] + first_ref[...].astype(jnp.float32)
    total += second_ref[...].astype(jnp.float32) + third_ref[...].astype(jnp.float32)
    next_ref[...] = total[:half]
    send_ref[...] = total[half:].astype(send_ref.dtype)
    done_ref[...] = token_ref[...]


def gather(keep, came, token):
    rows, width = keep.shape
    return call(
        gather_kernel,
        "gather",
        (
            pltpu.VMEM((rows // 2, width), jnp.float32),
            pltpu.VMEM((rows // 2, width), jnp.bfloat16),
            TOKEN,
        ),
        (in_vmem(keep),) + tuple(in_vmem(c) for c in came) + (in_vmem(token),),
        [VMEM] * 5,
    )


def close_kernel(
    experts, keep_ref, first_ref, second_ref, third_ref, residual_ref, routes_ref, gates_ref,
    token_ref, total_ref, send_ref, done_ref,
):
    done_ref[...] = token_ref[...]
    per, width = residual_ref.shape
    total = keep_ref[...] + first_ref[...].astype(jnp.float32)
    total += second_ref[...].astype(jnp.float32) + third_ref[...].astype(jnp.float32)
    own = total[:per] + residual_ref[...].astype(jnp.float32)
    total = jnp.concatenate([own, total[per:]], axis=0)
    lane = lax.broadcasted_iota(jnp.int32, (per, TABLE), 1)
    routes, gates = routes_ref[...], gates_ref[...]
    table = jnp.zeros((per, TABLE), jnp.float32)
    for t in range(routes.shape[1]):
        table += jnp.where(routes[:, t : t + 1] == lane % experts, gates[:, t : t + 1], 0.0)
    high = table.astype(jnp.bfloat16).astype(jnp.float32)
    middle = (table - high).astype(jnp.bfloat16).astype(jnp.float32)
    low = table - high - middle
    part = lane // experts
    table = jnp.where(
        part == 0, high, jnp.where(part == 1, middle, jnp.where(part == 2, low, 0.0))
    )
    table = jnp.concatenate([table, jnp.zeros_like(table)], axis=0)
    total_ref[:, :width] = total
    total_ref[:, width:] = table
    send_ref[:, :width] = total.astype(send_ref.dtype)
    send_ref[:, width:] = table.astype(send_ref.dtype)


def close(keep, came, residual, routes, gates, token, experts):
    rows, width = keep.shape
    shape = (rows, width + TABLE)
    return call(
        functools.partial(close_kernel, experts),
        "close",
        (pltpu.VMEM(shape, jnp.float32), pltpu.VMEM(shape, jnp.bfloat16), TOKEN),
        (in_vmem(keep),)
        + tuple(in_vmem(c) for c in came)
        + (residual, routes, gates, in_vmem(token)),
        [VMEM] * 8,
    )


def norm_kernel(total_ref, came_ref, gain_ref, token_ref, attended_ref, normed_ref, done_ref):
    done_ref[...] = token_ref[...]
    per, width = attended_ref.shape
    came = came_ref[...].astype(jnp.float32)
    total = total_ref[...] + jnp.concatenate([came[per:], came[:per]], axis=0)
    attended = total[:, :width].astype(jnp.bfloat16).astype(jnp.float32)
    attended_ref[...] = attended[:per].astype(jnp.bfloat16)
    mean = jnp.mean(attended * attended, axis=1, keepdims=True)
    normed = attended * lax.rsqrt(mean + 1e-06) * gain_ref[...]
    normed_ref[:, :width] = normed.astype(jnp.bfloat16)
    normed_ref[:, width:] = total[:, width:].astype(jnp.bfloat16)


def norm(total, came, gain, token, per):
    rows, width = total.shape
    return call(
        norm_kernel,
        "norm",
        (
            pltpu.VMEM((per, width - TABLE), jnp.bfloat16),
            pltpu.VMEM((rows, width), jnp.bfloat16),
            TOKEN,
        ),
        (in_vmem(total), in_vmem(came), gain.reshape(1, -1), in_vmem(token)),
        [VMEM] * 4,
    )


def expert_kernel(blocks, experts, me_ref, *refs):
    gate, up, first, down_hbm, token_ref, keep_ref, send_ref, done_ref, down, sems = refs[blocks:]
    early = first.shape[1]
    source = down_hbm.at[:, pl.ds(early, down.shape[1])]
    load = functools.partial(column_copy, source, down, sems)
    start_all(sems.shape[0], load)
    done_ref[...] = token_ref[...]
    model, units = gate.shape
    tile = down.shape[1] // sems.shape[0]
    half = keep_ref.shape[0]
    x = jnp.concatenate([r[...].astype(jnp.float32) for r in refs[:blocks]], axis=0)
    x = x.astype(jnp.bfloat16)
    table = x[:, model:].astype(jnp.float32)
    lane = lax.broadcasted_iota(jnp.int32, table.shape, 1)
    expert = (me_ref[0] * units) // FF_WIN
    mine = (lane % experts == expert) & (lane < 3 * experts)
    weight = jnp.sum(jnp.where(mine, table, 0.0), axis=1, keepdims=True)
    x = x[:, :model]
    rows = x.shape[0]
    x = tall(x)
    g = jnp.dot(x, gate[...], preferred_element_type=jnp.float32)[:rows]
    u = jnp.dot(x, up[...], preferred_element_type=jnp.float32)[:rows]
    act = tall((g / (1.0 + jnp.exp(-g)) * u).astype(jnp.bfloat16))

    def multiply(weights, at, to):
        y = jnp.dot(act, weights[:, at : at + tile], preferred_element_type=jnp.float32)
        y = y[:rows] * weight
        keep_ref[:, to : to + tile] = y[:half]
        send_ref[:, to : to + tile] = y[half:].astype(send_ref.dtype)

    for t in range(0, early, tile):
        multiply(first, t, t)
    for i in range(sems.shape[0]):
        load(i).wait()
        multiply(down, i * tile, early + i * tile)


def expert(me, blocks, gate, up, first, down, token, experts):
    model, units = gate.shape
    half = sum(b.shape[0] for b in blocks) // 2
    late = model - first.shape[1]
    return call(
        functools.partial(expert_kernel, len(blocks), experts),
        "expert",
        (
            pltpu.VMEM((half, model), jnp.float32),
            pltpu.VMEM((half, model), jnp.bfloat16),
            TOKEN,
        ),
        (me,)
        + tuple(in_vmem(b) for b in blocks)
        + (in_vmem(gate), in_vmem(up), in_vmem(first), in_hbm(down), in_vmem(token)),
        [SMEM] + [VMEM] * (len(blocks) + 3) + [HBM, VMEM],
        [
            pltpu.VMEM((units, late), down.dtype),
            pltpu.SemaphoreType.DMA((late // tile_of(late, 1024),)),
        ],
        limit=14,
    )


def last_kernel(keep_ref, came_ref, token_ref, out_ref):
    out_ref[...] = (keep_ref[...] + came_ref[...].astype(jnp.float32)).astype(out_ref.dtype)


def body(
    queries,
    latent_key_cache,
    lengths,
    value_up_weight,
    out_proj,
    residual_in,
    norm_gain,
    w_gate,
    w_up,
    w_down,
    routes,
    route_gates,
):
    devices = lax.axis_size("exp")
    bits = devices.bit_length() - 1
    per = queries.shape[0]
    experts = devices * w_gate.shape[1] // FF_WIN
    me = lax.axis_index("exp").astype(jnp.int32).reshape(1)

    def swap(x, *some_bits):
        mask = sum(1 << bit for bit in some_bits)
        return lax.ppermute(x, "exp", [(i, i ^ mask) for i in range(devices)])

    def square(sends):
        low, high = bits - 3, bits - 2
        return swap(sends[0], high), swap(sends[1], low), swap(sends[2], low, high)

    early = out_proj.shape[1] // 7 * 6
    token = jnp.zeros(TOKEN.shape, TOKEN.dtype)
    if bits == 4:
        own, send = attend(me, queries, latent_key_cache, lengths, bits, 2)
        own, *sends, token = pack(own, swap(send, 0), token)
        keep, send, token = split((own,) + square(sends), token)
        came = swap(send, 3)
        first, token = load(token, out_proj, early)
        latents = [keep, came]
    else:
        (latent,) = attend(me, queries, latent_key_cache, lengths, bits, 1)
        latents = [lax.all_to_all(latent, "exp", split_axis=0, concat_axis=0, tiled=True)]
        first, token = load(token, out_proj, early)
    latents = [x.reshape(-1, LATENT_WIDTH) for x in latents]
    keep, send = project(me, latents, value_up_weight, out_proj, first, per, bits)
    for bit in range(bits - 4):
        keep, send, token = fold(keep, swap(send, bit), token)
    keep, *sends, token = fold(keep, swap(send, bits - 4), token, 4)
    came = square(sends)
    total, send, token = close(keep, came, residual_in, routes, route_gates, token, experts)
    came = swap(send, bits - 1)
    first, token = load(token, w_down, w_down.shape[1] // 7 * 2)
    attended, x, token = norm(total, came, norm_gain, token, per)
    for bit in reversed(range(bits - 1)):
        if bit > 2:
            x = jnp.concatenate([x, swap(x, bit)], axis=0)
        elif bit == 2:
            blocks = [x, swap(x, 2), swap(x, 1), swap(x, 2, 1)]
        elif bit == 0:
            blocks = blocks + [swap(b, 0) for b in blocks]
    keep, send, token = expert(me, blocks, w_gate, w_up, first, w_down, token, experts)
    for bit in range(bits - 4):
        keep, send, token = fold(keep, swap(send, bit), token)
    keep, *sends, token = fold(keep, swap(send, bits - 4), token, 4)
    keep, send, token = gather(keep, square(sends), token)
    (mixed,) = call(
        last_kernel,
        "last",
        (jax.ShapeDtypeStruct(attended.shape, jnp.bfloat16),),
        (in_vmem(keep), in_vmem(swap(send, bits - 1)), in_vmem(token)),
        [VMEM] * 3,
    )
    return attended, mixed


def solution(mesh):
    placed = (
        P(("grp", "exp"), None, None),
        P(("grp", "exp"), None, None),
        P(("grp", "exp")),
        P("exp", None, None),
        P("exp", None),
        P(("grp", "exp"), None),
        P(),
        P(None, "exp"),
        P(None, "exp"),
        P("exp", None),
        P(("grp", "exp"), None),
        P(("grp", "exp"), None),
    )
    return jax.shard_map(
        body,
        mesh=mesh,
        in_specs=placed,
        out_specs=(P(("grp", "exp"), None), P(("grp", "exp"), None)),
        check_vma=False,
    )
```

```python
import functools

import jax
import jax.numpy as jnp
from jax import lax
from jax.experimental import pallas as pl
from jax.experimental.pallas import tpu as pltpu
from jax.sharding import PartitionSpec as P

LATENT_WIDTH = 512
ROTARY_WIDTH = 64
HEAD_VALUE_WIDTH = 128
FF_WIN = 1024
TABLE = 128
MIB = 1 << 20

HBM = pl.BlockSpec(memory_space=pl.ANY)
VMEM = pl.BlockSpec(memory_space=pltpu.VMEM)
SMEM = pl.BlockSpec(memory_space=pltpu.SMEM)


def tile_of(extent, wanted):
    while extent % wanted:
        wanted //= 2
    return wanted


def in_hbm(x):
    return pltpu.with_memory_space_constraint(x, pltpu.HBM)


def in_vmem(x):
    return pltpu.with_memory_space_constraint(x, pltpu.VMEM)


TOKEN = pltpu.VMEM((8, 128), jnp.float32)


def tall(x):
    rows = x.shape[0]
    if rows >= 128:
        return x
    return jnp.concatenate([x, jnp.zeros((128 - rows, x.shape[1]), x.dtype)], axis=0)


def call(kernel, name, outs, ins, specs, scratch=(), limit=4, moved=None):
    cost = None
    if moved:
        cost = pl.CostEstimate(flops=0, bytes_accessed=moved, transcendentals=0)
    return pl.pallas_call(
        kernel,
        out_shape=outs,
        in_specs=specs,
        out_specs=tuple(VMEM for _ in outs),
        scratch_shapes=list(scratch),
        compiler_params=pltpu.CompilerParams(vmem_limit_bytes=limit * MIB),
        cost_estimate=cost,
        name=name,
    )(*ins)


def row_copy(source, target, sems, i):
    rows = source.shape[0] // sems.shape[0]
    at = pl.ds(pl.multiple_of(i * rows, rows), rows)
    return pltpu.make_async_copy(source.at[at], target.at[at], sems.at[i])


def column_copy(source, target, sems, i):
    tile = source.shape[1] // sems.shape[0]
    at = pl.ds(pl.multiple_of(i * tile, tile), tile)
    return pltpu.make_async_copy(source.at[:, at], target.at[:, at], sems.at[i])


def start_all(count, copy):
    def step(i, carry):
        copy(i).start()
        return carry

    lax.fori_loop(0, count, step, 0)


LOADS = 4


def load_kernel(start, token_ref, source, target, done_ref, sems):
    source = source.at[:, pl.ds(start, target.shape[1])]
    copies = [row_copy(source, target, sems, part) for part in range(LOADS)]
    for c in copies:
        c.start()
    done_ref[...] = token_ref[...]
    for c in copies:
        c.wait()


def load(token, weight, columns, start=0):
    return call(
        functools.partial(load_kernel, start),
        "load",
        (pltpu.VMEM((weight.shape[0], columns), weight.dtype), TOKEN),
        (in_vmem(token), in_hbm(weight)),
        [VMEM, HBM],
        [pltpu.SemaphoreType.DMA((LOADS,))],
        limit=2,
        moved=weight.shape[0] * columns * 2,
    )


def attend_kernel(
    bits, me_ref, lengths_hbm, q_hbm, cache_hbm, *refs
):
    outs = refs[:-5]
    lengths, queries, cache, sems, small_sems = refs[-5:]
    requests, width, length = cache.shape
    chunks = sems.shape[1]
    chunk = length // chunks
    latent = outs[0].shape[-1]
    heads = queries.shape[2]
    here = heads >> bits
    scale = (HEAD_VALUE_WIDTH + ROTARY_WIDTH) ** (-0.5)

    def copy(r, c):
        at = pl.ds(pl.multiple_of(c * chunk, chunk), chunk)
        return pltpu.make_async_copy(
            cache_hbm.at[r, :, at], cache.at[r, :, at], sems.at[r, c]
        )

    first = [
        pltpu.make_async_copy(lengths_hbm, lengths, small_sems.at[0]),
        pltpu.make_async_copy(q_hbm, queries, small_sems.at[1]),
    ]
    for c in first:
        c.start()
    for r in range(requests):
        start_all(chunks, functools.partial(copy, r))
    for c in first:
        c.wait()
    at = me_ref[0] if len(outs) == 2 else None
    order = one_hot(row_order(at, heads, here, bits))
    scores = []
    for r in range(requests):
        q = lax.dot_general(
            order,
            queries[r],
            (((1,), (1,)), ((), ())),
            preferred_element_type=jnp.float32,
        ).astype(jnp.bfloat16)
        parts = []
        for c in range(chunks):
            copy(r, c).wait()
            s = jnp.dot(
                q,
                cache[r, :, c * chunk : (c + 1) * chunk],
                preferred_element_type=jnp.float32,
            )
            at = lax.broadcasted_iota(jnp.int32, s.shape, 1) + c * chunk
            parts.append(jnp.where(at < lengths[r], s * scale, -jnp.inf))
        scores.append(jnp.concatenate(parts, axis=1))
    results = []
    for r in range(requests):
        peak = jnp.max(scores[r], axis=1, keepdims=True)
        e = jnp.exp(scores[r] - peak)
        p = (e * (1.0 / jnp.sum(e, axis=1, keepdims=True))).astype(jnp.bfloat16)
        o = lax.dot_general(
            p,
            cache[r, :latent, :],
            (((1,), (1,)), ((), ())),
            preferred_element_type=jnp.float32,
        )
        results.append(o.reshape(1 << bits, here, latent))
    out = jnp.concatenate(results, axis=1).astype(jnp.bfloat16)
    share = (1 << bits) // len(outs)
    for i, ref in enumerate(outs):
        ref[...] = out[i * share : (i + 1) * share]


def attend(me, queries, cache, lengths, bits, sides):
    requests, heads, width = queries.shape
    length = cache.shape[1]
    devices = 1 << bits
    slots = requests * heads // devices
    chunks = length // tile_of(length, 1024)
    return call(
        functools.partial(attend_kernel, bits),
        "attend",
        (pltpu.VMEM((devices // sides, slots, LATENT_WIDTH), jnp.bfloat16),) * sides,
        (
            me,
            in_hbm(lengths),
            in_hbm(jnp.swapaxes(queries, 1, 2)),
            in_hbm(jnp.swapaxes(cache, 1, 2)),
        ),
        [SMEM] + [HBM] * 3,
        [
            pltpu.SMEM((requests,), jnp.int32),
            pltpu.VMEM((requests, width, heads), jnp.bfloat16),
            pltpu.VMEM((requests, width, length), jnp.bfloat16),
            pltpu.SemaphoreType.DMA((requests, chunks)),
            pltpu.SemaphoreType.DMA((2,)),
        ],
        limit=16,
    )


def pack_kernel(own_ref, came_ref, token_ref, *refs):
    *outs, done_ref = refs
    for i, ref in enumerate(outs):
        for far in range(2):
            ref[far, 0] = own_ref[2 * i + far]
            ref[far, 1] = came_ref[2 * i + far]
    done_ref[...] = token_ref[...]


def pack(own, came, token):
    shape = (2, 2) + own.shape[1:]
    return call(
        pack_kernel,
        "pack",
        (pltpu.VMEM(shape, own.dtype),) * 4 + (TOKEN,),
        (in_vmem(own), in_vmem(came), in_vmem(token)),
        [VMEM] * 3,
    )


def split_kernel(*refs):
    *sources, token_ref, keep_ref, send_ref, done_ref = refs
    for i, ref in enumerate(sources):
        keep_ref[i] = ref[0]
        send_ref[i] = ref[1]
    done_ref[...] = token_ref[...]


def split(blocks, token):
    shape = (len(blocks),) + blocks[0].shape[1:]
    return call(
        split_kernel,
        "split",
        (pltpu.VMEM(shape, blocks[0].dtype),) * 2 + (TOKEN,),
        tuple(in_vmem(b) for b in blocks) + (in_vmem(token),),
        [VMEM] * (len(blocks) + 1),
    )


def relative(index, bits):
    out = jnp.zeros_like(index)
    for b in range(bits):
        out = out | (((index >> b) & 1) << (bits - 1 - b))
    return out


def row_order(me, rows, per, bits):
    i = lax.broadcasted_iota(jnp.int32, (rows, rows), 0)
    j = lax.broadcasted_iota(jnp.int32, (rows, rows), 1)
    if me is None:
        return i == j
    shift = per.bit_length() - 1
    owner = relative(i >> shift, bits) ^ me
    return j == (owner << shift) + (i & (per - 1))


def square_order(rows, per):
    i = lax.broadcasted_iota(jnp.int32, (rows, rows), 0)
    j = lax.broadcasted_iota(jnp.int32, (rows, rows), 1)
    shift = per.bit_length() - 1
    q = i >> shift
    owner = ((q & 1) << 3) | (q & 6) | (q >> 3)
    return j == (owner << shift) + (i & (per - 1))


def one_hot(order):
    return jnp.where(order, 1.0, 0.0).astype(jnp.bfloat16)


def project_kernel(
    bits, per, me_ref, up_ref, proj_hbm, first, *refs
):
    *latents, keep_ref, send_ref, rest, sems = refs
    tile = rest.shape[1] // sems.shape[0]
    early = first.shape[1]
    source = proj_hbm.at[:, pl.ds(early, rest.shape[1])]
    load = functools.partial(column_copy, source, rest, sems)
    start_all(sems.shape[0], load)
    heads, latent, value = up_ref.shape
    x = jnp.concatenate([ref[...] for ref in latents], axis=0)
    rows = x.shape[0] // heads
    half = rows // 2
    parts = []
    together = min(2, heads)
    for h in range(0, heads, together):
        up = jnp.concatenate([up_ref[h + i] for i in range(together)], axis=1)
        y = jnp.dot(x, up, preferred_element_type=jnp.float32)
        y = y.reshape(rows, heads, together * value)
        head = lax.broadcasted_iota(jnp.int32, y.shape, 1)
        lane = lax.broadcasted_iota(jnp.int32, y.shape, 2)
        parts.append(jnp.sum(jnp.where(head == h + lane // value, y, 0.0), axis=1))
    values = jnp.concatenate(parts, axis=1).astype(jnp.bfloat16)
    if len(latents) == 2:
        order = square_order(rows, per)
    else:
        order = row_order(me_ref[0], rows, per, bits)
    values = jnp.dot(one_hot(order), values, preferred_element_type=jnp.float32).astype(jnp.bfloat16)
    values = tall(values)

    def multiply(weights, at, to):
        y = jnp.dot(values, weights[:, at : at + tile], preferred_element_type=jnp.float32)
        keep_ref[:, to : to + tile] = y[:half]
        send_ref[:, to : to + tile] = y[half:rows].astype(send_ref.dtype)

    for t in range(0, early, tile):
        multiply(first, t, t)
    for i in range(sems.shape[0]):
        load(i).wait()
        multiply(rest, i * tile, early + i * tile)


def project(me, latents, up, proj, first, per, bits):
    depth, width = proj.shape
    late = width - first.shape[1]
    half = sum(x.shape[0] for x in latents) // up.shape[0] // 2
    return call(
        functools.partial(project_kernel, bits, per),
        "project",
        (pltpu.VMEM((half, width), jnp.float32), pltpu.VMEM((half, width), jnp.bfloat16)),
        (me, in_vmem(up), in_hbm(proj), in_vmem(first)) + tuple(in_vmem(x) for x in latents),
        [SMEM, VMEM, HBM, VMEM] + [VMEM] * len(latents),
        [
            pltpu.VMEM((depth, late), proj.dtype),
            pltpu.SemaphoreType.DMA((late // tile_of(late, 512),)),
        ],
        limit=6,
        moved=100 * MIB,
    )


def fold_kernel(parts, keep_ref, came_ref, *refs):
    rows = keep_ref.shape[0] // parts
    outs = refs[len(refs) - parts - 1 :]
    total = keep_ref[...] + came_ref[...].astype(jnp.float32)
    outs[0][...] = total[:rows]
    for i in range(1, parts):
        outs[i][...] = total[i * rows : (i + 1) * rows].astype(outs[i].dtype)
    outs[parts][...] = refs[0][...]


def fold(keep, came, token, parts=2):
    rows, width = keep.shape
    return call(
        functools.partial(fold_kernel, parts),
        "fold",
        (pltpu.VMEM((rows // parts, width), jnp.float32),)
        + (pltpu.VMEM((rows // parts, width), jnp.bfloat16),) * (parts - 1)
        + (TOKEN,),
        (in_vmem(keep), in_vmem(came), in_vmem(token)),
        [VMEM] * 3,
    )


def gather_kernel(keep_ref, first_ref, second_ref, third_ref, token_ref, next_ref, send_ref, done_ref):
    half = next_ref.shape[0]
    total = keep_ref[...] + first_ref[...].astype(jnp.float32)
    total += second_ref[...].astype(jnp.float32) + third_ref[...].astype(jnp.float32)
    next_ref[...] = total[:half]
    send_ref[...] = total[half:].astype(send_ref.dtype)
    done_ref[...] = token_ref[...]


def gather(keep, came, token):
    rows, width = keep.shape
    return call(
        gather_kernel,
        "gather",
        (
            pltpu.VMEM((rows // 2, width), jnp.float32),
            pltpu.VMEM((rows // 2, width), jnp.bfloat16),
            TOKEN,
        ),
        (in_vmem(keep),) + tuple(in_vmem(c) for c in came) + (in_vmem(token),),
        [VMEM] * 5,
    )


def close_kernel(
    experts, keep_ref, first_ref, second_ref, third_ref, residual_ref, routes_ref, gates_ref,
    token_ref, total_ref, send_ref, done_ref,
):
    done_ref[...] = token_ref[...]
    per, width = residual_ref.shape
    total = keep_ref[...] + first_ref[...].astype(jnp.float32)
    total += second_ref[...].astype(jnp.float32) + third_ref[...].astype(jnp.float32)
    own = total[:per] + residual_ref[...].astype(jnp.float32)
    total = jnp.concatenate([own, total[per:]], axis=0)
    lane = lax.broadcasted_iota(jnp.int32, (per, TABLE), 1)
    routes, gates = routes_ref[...], gates_ref[...]
    table = jnp.zeros((per, TABLE), jnp.float32)
    for t in range(routes.shape[1]):
        table += jnp.where(routes[:, t : t + 1] == lane % experts, gates[:, t : t + 1], 0.0)
    high = table.astype(jnp.bfloat16).astype(jnp.float32)
    middle = (table - high).astype(jnp.bfloat16).astype(jnp.float32)
    low = table - high - middle
    part = lane // experts
    table = jnp.where(
        part == 0, high, jnp.where(part == 1, middle, jnp.where(part == 2, low, 0.0))
    )
    table = jnp.concatenate([table, jnp.zeros_like(table)], axis=0)
    total_ref[:, :width] = total
    total_ref[:, width:] = table
    send_ref[:, :width] = total.astype(send_ref.dtype)
    send_ref[:, width:] = table.astype(send_ref.dtype)


def close(keep, came, residual, routes, gates, token, experts):
    rows, width = keep.shape
    shape = (rows, width + TABLE)
    return call(
        functools.partial(close_kernel, experts),
        "close",
        (pltpu.VMEM(shape, jnp.float32), pltpu.VMEM(shape, jnp.bfloat16), TOKEN),
        (in_vmem(keep),)
        + tuple(in_vmem(c) for c in came)
        + (residual, routes, gates, in_vmem(token)),
        [VMEM] * 8,
    )


def norm_kernel(total_ref, came_ref, gain_ref, token_ref, attended_ref, normed_ref, done_ref):
    done_ref[...] = token_ref[...]
    per, width = attended_ref.shape
    came = came_ref[...].astype(jnp.float32)
    total = total_ref[...] + jnp.concatenate([came[per:], came[:per]], axis=0)
    attended = total[:, :width].astype(jnp.bfloat16).astype(jnp.float32)
    attended_ref[...] = attended[:per].astype(jnp.bfloat16)
    mean = jnp.mean(attended * attended, axis=1, keepdims=True)
    normed = attended * lax.rsqrt(mean + 1e-06) * gain_ref[...]
    normed_ref[:, :width] = normed.astype(jnp.bfloat16)
    normed_ref[:, width:] = total[:, width:].astype(jnp.bfloat16)


def norm(total, came, gain, token, per):
    rows, width = total.shape
    return call(
        norm_kernel,
        "norm",
        (
            pltpu.VMEM((per, width - TABLE), jnp.bfloat16),
            pltpu.VMEM((rows, width), jnp.bfloat16),
            TOKEN,
        ),
        (in_vmem(total), in_vmem(came), gain.reshape(1, -1), in_vmem(token)),
        [VMEM] * 4,
    )


def expert_kernel(blocks, experts, me_ref, *refs):
    gate, up, *firsts, down_hbm, token_ref, keep_ref, send_ref, done_ref, down, sems = refs[blocks:]
    early = sum(first.shape[1] for first in firsts)
    source = down_hbm.at[:, pl.ds(early, down.shape[1])]
    load = functools.partial(column_copy, source, down, sems)
    start_all(sems.shape[0], load)
    done_ref[...] = token_ref[...]
    model, units = gate.shape
    tile = down.shape[1] // sems.shape[0]
    half = keep_ref.shape[0]
    x = jnp.concatenate([r[...].astype(jnp.float32) for r in refs[:blocks]], axis=0)
    x = x.astype(jnp.bfloat16)
    table = x[:, model:].astype(jnp.float32)
    lane = lax.broadcasted_iota(jnp.int32, table.shape, 1)
    expert = (me_ref[0] * units) // FF_WIN
    mine = (lane % experts == expert) & (lane < 3 * experts)
    weight = jnp.sum(jnp.where(mine, table, 0.0), axis=1, keepdims=True)
    x = x[:, :model]
    rows = x.shape[0]
    x = tall(x)
    g = jnp.dot(x, gate[...], preferred_element_type=jnp.float32)[:rows]
    u = jnp.dot(x, up[...], preferred_element_type=jnp.float32)[:rows]
    act = tall((g / (1.0 + jnp.exp(-g)) * u).astype(jnp.bfloat16))

    def multiply(weights, at, to):
        y = jnp.dot(act, weights[:, at : at + tile], preferred_element_type=jnp.float32)
        y = y[:rows] * weight
        keep_ref[:, to : to + tile] = y[:half]
        send_ref[:, to : to + tile] = y[half:].astype(send_ref.dtype)

    to = 0
    for first in firsts:
        for t in range(0, first.shape[1], tile):
            multiply(first, t, to + t)
        to += first.shape[1]
    for i in range(sems.shape[0]):
        load(i).wait()
        multiply(down, i * tile, early + i * tile)


def expert(me, blocks, gate, up, firsts, down, token, experts):
    model, units = gate.shape
    half = sum(b.shape[0] for b in blocks) // 2
    late = model - sum(first.shape[1] for first in firsts)
    return call(
        functools.partial(expert_kernel, len(blocks), experts),
        "expert",
        (
            pltpu.VMEM((half, model), jnp.float32),
            pltpu.VMEM((half, model), jnp.bfloat16),
            TOKEN,
        ),
        (me,)
        + tuple(in_vmem(b) for b in blocks)
        + tuple(in_vmem(w) for w in (gate, up, *firsts))
        + (in_hbm(down), in_vmem(token)),
        [SMEM] + [VMEM] * (len(blocks) + 2 + len(firsts)) + [HBM, VMEM],
        [
            pltpu.VMEM((units, late), down.dtype),
            pltpu.SemaphoreType.DMA((late // tile_of(late, 1024),)),
        ],
        limit=10,
    )


def last_kernel(keep_ref, came_ref, token_ref, out_ref):
    out_ref[...] = (keep_ref[...] + came_ref[...].astype(jnp.float32)).astype(out_ref.dtype)


def body(
    queries,
    latent_key_cache,
    lengths,
    value_up_weight,
    out_proj,
    residual_in,
    norm_gain,
    w_gate,
    w_up,
    w_down,
    routes,
    route_gates,
):
    devices = lax.axis_size("exp")
    bits = devices.bit_length() - 1
    per = queries.shape[0]
    experts = devices * w_gate.shape[1] // FF_WIN
    me = lax.axis_index("exp").astype(jnp.int32).reshape(1)

    def swap(x, *some_bits):
        mask = sum(1 << bit for bit in some_bits)
        return lax.ppermute(x, "exp", [(i, i ^ mask) for i in range(devices)])

    def square(sends):
        low, high = bits - 3, bits - 2
        return swap(sends[0], high), swap(sends[1], low), swap(sends[2], low, high)

    early = out_proj.shape[1] // 7 * 6
    token = jnp.zeros(TOKEN.shape, TOKEN.dtype)
    if bits == 4:
        own, send = attend(me, queries, latent_key_cache, lengths, bits, 2)
        own, *sends, token = pack(own, swap(send, 0), token)
        keep, send, token = split((own,) + square(sends), token)
        came = swap(send, 3)
        first, token = load(token, out_proj, early)
        latents = [keep, came]
    else:
        (latent,) = attend(me, queries, latent_key_cache, lengths, bits, 1)
        latents = [lax.all_to_all(latent, "exp", split_axis=0, concat_axis=0, tiled=True)]
        first, token = load(token, out_proj, early)
    latents = [x.reshape(-1, LATENT_WIDTH) for x in latents]
    keep, send = project(me, latents, value_up_weight, out_proj, first, per, bits)
    for bit in range(bits - 4):
        keep, send, token = fold(keep, swap(send, bit), token)
    keep, *sends, token = fold(keep, swap(send, bits - 4), token, 4)
    came = square(sends)
    part = w_down.shape[1] // 7
    first, token = load(token, w_down, 2 * part)
    total, send, token = close(keep, came, residual_in, routes, route_gates, token, experts)
    came = swap(send, bits - 1)
    second, token = load(token, w_down, 2 * part, 2 * part)
    attended, x, token = norm(total, came, norm_gain, token, per)
    for bit in reversed(range(bits - 1)):
        if bit > 2:
            x = jnp.concatenate([x, swap(x, bit)], axis=0)
        elif bit == 2:
            blocks = [x, swap(x, 2), swap(x, 1), swap(x, 2, 1)]
        elif bit == 0:
            blocks = blocks + [swap(b, 0) for b in blocks]
    keep, send, token = expert(me, blocks, w_gate, w_up, [first, second], w_down, token, experts)
    for bit in range(bits - 4):
        keep, send, token = fold(keep, swap(send, bit), token)
    keep, *sends, token = fold(keep, swap(send, bits - 4), token, 4)
    keep, send, token = gather(keep, square(sends), token)
    (mixed,) = call(
        last_kernel,
        "last",
        (jax.ShapeDtypeStruct(attended.shape, jnp.bfloat16),),
        (in_vmem(keep), in_vmem(swap(send, bits - 1)), in_vmem(token)),
        [VMEM] * 3,
    )
    return attended, mixed


def solution(mesh):
    placed = (
        P(("grp", "exp"), None, None),
        P(("grp", "exp"), None, None),
        P(("grp", "exp")),
        P("exp", None, None),
        P("exp", None),
        P(("grp", "exp"), None),
        P(),
        P(None, "exp"),
        P(None, "exp"),
        P("exp", None),
        P(("grp", "exp"), None),
        P(("grp", "exp"), None),
    )
    return jax.shard_map(
        body,
        mesh=mesh,
        in_specs=placed,
        out_specs=(P(("grp", "exp"), None), P(("grp", "exp"), None)),
        check_vma=False,
    )
```

```python
import functools

import jax
import jax.numpy as jnp
from jax import lax
from jax.experimental import pallas as pl
from jax.experimental.pallas import tpu as pltpu
from jax.sharding import PartitionSpec as P

LATENT_WIDTH = 512
ROTARY_WIDTH = 64
HEAD_VALUE_WIDTH = 128
FF_WIN = 1024
TABLE = 128
MIB = 1 << 20

HBM = pl.BlockSpec(memory_space=pl.ANY)
VMEM = pl.BlockSpec(memory_space=pltpu.VMEM)
SMEM = pl.BlockSpec(memory_space=pltpu.SMEM)


def tile_of(extent, wanted):
    while extent % wanted:
        wanted //= 2
    return wanted


def in_hbm(x):
    return pltpu.with_memory_space_constraint(x, pltpu.HBM)


def in_vmem(x):
    return pltpu.with_memory_space_constraint(x, pltpu.VMEM)


TOKEN = pltpu.VMEM((8, 128), jnp.float32)


def tall(x):
    rows = x.shape[0]
    if rows >= 128:
        return x
    return jnp.concatenate([x, jnp.zeros((128 - rows, x.shape[1]), x.dtype)], axis=0)


def call(kernel, name, outs, ins, specs, scratch=(), limit=4, moved=None):
    cost = None
    if moved:
        cost = pl.CostEstimate(flops=0, bytes_accessed=moved, transcendentals=0)
    return pl.pallas_call(
        kernel,
        out_shape=outs,
        in_specs=specs,
        out_specs=tuple(VMEM for _ in outs),
        scratch_shapes=list(scratch),
        compiler_params=pltpu.CompilerParams(vmem_limit_bytes=limit * MIB),
        cost_estimate=cost,
        name=name,
    )(*ins)


def row_copy(source, target, sems, i):
    rows = source.shape[0] // sems.shape[0]
    at = pl.ds(pl.multiple_of(i * rows, rows), rows)
    return pltpu.make_async_copy(source.at[at], target.at[at], sems.at[i])


def column_copy(source, target, sems, i):
    tile = source.shape[1] // sems.shape[0]
    at = pl.ds(pl.multiple_of(i * tile, tile), tile)
    return pltpu.make_async_copy(source.at[:, at], target.at[:, at], sems.at[i])


def start_all(count, copy):
    def step(i, carry):
        copy(i).start()
        return carry

    lax.fori_loop(0, count, step, 0)


LOADS = 4


def load_kernel(start, token_ref, source, target, done_ref, sems):
    source = source.at[:, pl.ds(start, target.shape[1])]
    copies = [row_copy(source, target, sems, part) for part in range(LOADS)]
    for c in copies:
        c.start()
    done_ref[...] = token_ref[...]
    for c in copies:
        c.wait()


def load(token, weight, columns, start=0):
    return call(
        functools.partial(load_kernel, start),
        "load",
        (pltpu.VMEM((weight.shape[0], columns), weight.dtype), TOKEN),
        (in_vmem(token), in_hbm(weight)),
        [VMEM, HBM],
        [pltpu.SemaphoreType.DMA((LOADS,))],
        limit=2,
        moved=weight.shape[0] * columns * 2,
    )


def attend_kernel(
    bits, me_ref, lengths_hbm, q_hbm, cache_hbm, proj_hbm, *refs
):
    *outs, proj, lengths, queries, cache, sems, small_sems, proj_sems = refs
    load = functools.partial(
        row_copy, proj_hbm.at[:, pl.ds(0, proj.shape[1])], proj, proj_sems
    )
    requests, width, length = cache.shape
    chunks = sems.shape[1]
    chunk = length // chunks
    latent = outs[0].shape[-1]
    heads = queries.shape[2]
    here = heads >> bits
    scale = (HEAD_VALUE_WIDTH + ROTARY_WIDTH) ** (-0.5)

    def copy(r, c):
        at = pl.ds(pl.multiple_of(c * chunk, chunk), chunk)
        return pltpu.make_async_copy(
            cache_hbm.at[r, :, at], cache.at[r, :, at], sems.at[r, c]
        )

    first = [
        pltpu.make_async_copy(lengths_hbm, lengths, small_sems.at[0]),
        pltpu.make_async_copy(q_hbm, queries, small_sems.at[1]),
    ]
    for c in first:
        c.start()
    for r in range(requests):
        start_all(chunks, functools.partial(copy, r))
    for c in first:
        c.wait()
    order = one_hot(row_order(None, heads, here, bits))
    scores = []
    for r in range(requests):
        q = lax.dot_general(
            order,
            queries[r],
            (((1,), (1,)), ((), ())),
            preferred_element_type=jnp.float32,
        ).astype(jnp.bfloat16)
        parts = []
        for c in range(chunks):
            copy(r, c).wait()
            s = jnp.dot(
                q,
                cache[r, :, c * chunk : (c + 1) * chunk],
                preferred_element_type=jnp.float32,
            )
            at = lax.broadcasted_iota(jnp.int32, s.shape, 1) + c * chunk
            parts.append(jnp.where(at < lengths[r], s * scale, -jnp.inf))
        scores.append(jnp.concatenate(parts, axis=1))
        if r == 0:
            start_all(LOADS, load)
    results = []
    for r in range(requests):
        peak = jnp.max(scores[r], axis=1, keepdims=True)
        e = jnp.exp(scores[r] - peak)
        p = (e * (1.0 / jnp.sum(e, axis=1, keepdims=True))).astype(jnp.bfloat16)
        o = lax.dot_general(
            p,
            cache[r, :latent, :],
            (((1,), (1,)), ((), ())),
            preferred_element_type=jnp.float32,
        )
        results.append(o.reshape(1 << bits, here, latent))
    out = jnp.concatenate(results, axis=1).astype(jnp.bfloat16)
    share = (1 << bits) // len(outs)
    for i, ref in enumerate(outs):
        ref[...] = out[i * share : (i + 1) * share]
    for i in range(LOADS):
        load(i).wait()


def attend(me, queries, cache, lengths, proj, early, bits):
    sides = 1
    requests, heads, width = queries.shape
    length = cache.shape[1]
    devices = 1 << bits
    slots = requests * heads // devices
    chunks = length // tile_of(length, 1024)
    return call(
        functools.partial(attend_kernel, bits),
        "attend",
        (
            pltpu.VMEM((devices // sides, slots, LATENT_WIDTH), jnp.bfloat16),
            pltpu.VMEM((proj.shape[0], early), proj.dtype),
        ),
        (
            me,
            in_hbm(lengths),
            in_hbm(jnp.swapaxes(queries, 1, 2)),
            in_hbm(jnp.swapaxes(cache, 1, 2)),
            in_hbm(proj),
        ),
        [SMEM] + [HBM] * 4,
        [
            pltpu.SMEM((requests,), jnp.int32),
            pltpu.VMEM((requests, width, heads), jnp.bfloat16),
            pltpu.VMEM((requests, width, length), jnp.bfloat16),
            pltpu.SemaphoreType.DMA((requests, chunks)),
            pltpu.SemaphoreType.DMA((2,)),
            pltpu.SemaphoreType.DMA((LOADS,)),
        ],
        limit=16,
    )


def relative(index, bits):
    out = jnp.zeros_like(index)
    for b in range(bits):
        out = out | (((index >> b) & 1) << (bits - 1 - b))
    return out


def row_order(me, rows, per, bits):
    i = lax.broadcasted_iota(jnp.int32, (rows, rows), 0)
    j = lax.broadcasted_iota(jnp.int32, (rows, rows), 1)
    if me is None:
        return i == j
    shift = per.bit_length() - 1
    owner = relative(i >> shift, bits) ^ me
    return j == (owner << shift) + (i & (per - 1))


def one_hot(order):
    return jnp.where(order, 1.0, 0.0).astype(jnp.bfloat16)


def project_kernel(
    bits, per, me_ref, up_ref, proj_hbm, first, *refs
):
    *latents, keep_ref, send_ref, rest, sems = refs
    tile = rest.shape[1] // sems.shape[0]
    early = first.shape[1]
    source = proj_hbm.at[:, pl.ds(early, rest.shape[1])]
    load = functools.partial(column_copy, source, rest, sems)
    start_all(sems.shape[0], load)
    heads, latent, value = up_ref.shape
    x = jnp.concatenate([ref[...] for ref in latents], axis=0)
    rows = x.shape[0] // heads
    half = rows // 2
    parts = []
    together = min(2, heads)
    for h in range(0, heads, together):
        up = jnp.concatenate([up_ref[h + i] for i in range(together)], axis=1)
        y = jnp.dot(x, up, preferred_element_type=jnp.float32)
        y = y.reshape(rows, heads, together * value)
        head = lax.broadcasted_iota(jnp.int32, y.shape, 1)
        lane = lax.broadcasted_iota(jnp.int32, y.shape, 2)
        parts.append(jnp.sum(jnp.where(head == h + lane // value, y, 0.0), axis=1))
    values = jnp.concatenate(parts, axis=1).astype(jnp.bfloat16)
    order = row_order(me_ref[0], rows, per, bits)
    values = jnp.dot(one_hot(order), values, preferred_element_type=jnp.float32).astype(jnp.bfloat16)
    values = tall(values)

    def multiply(weights, at, to):
        y = jnp.dot(values, weights[:, at : at + tile], preferred_element_type=jnp.float32)
        keep_ref[:, to : to + tile] = y[:half]
        send_ref[:, to : to + tile] = y[half:rows].astype(send_ref.dtype)

    for t in range(0, early, tile):
        multiply(first, t, t)
    for i in range(sems.shape[0]):
        load(i).wait()
        multiply(rest, i * tile, early + i * tile)


def project(me, latents, up, proj, first, per, bits):
    depth, width = proj.shape
    late = width - first.shape[1]
    half = sum(x.shape[0] for x in latents) // up.shape[0] // 2
    return call(
        functools.partial(project_kernel, bits, per),
        "project",
        (pltpu.VMEM((half, width), jnp.float32), pltpu.VMEM((half, width), jnp.bfloat16)),
        (me, in_vmem(up), in_hbm(proj), in_vmem(first)) + tuple(in_vmem(x) for x in latents),
        [SMEM, VMEM, HBM, VMEM] + [VMEM] * len(latents),
        [
            pltpu.VMEM((depth, late), proj.dtype),
            pltpu.SemaphoreType.DMA((late // tile_of(late, 512),)),
        ],
        limit=14,
        moved=100 * MIB,
    )


def fold_kernel(parts, keep_ref, came_ref, *refs):
    rows = keep_ref.shape[0] // parts
    outs = refs[len(refs) - parts - 1 :]
    total = keep_ref[...] + came_ref[...].astype(jnp.float32)
    outs[0][...] = total[:rows]
    for i in range(1, parts):
        outs[i][...] = total[i * rows : (i + 1) * rows].astype(outs[i].dtype)
    outs[parts][...] = refs[0][...]


def fold(keep, came, token, parts=2):
    rows, width = keep.shape
    return call(
        functools.partial(fold_kernel, parts),
        "fold",
        (pltpu.VMEM((rows // parts, width), jnp.float32),)
        + (pltpu.VMEM((rows // parts, width), jnp.bfloat16),) * (parts - 1)
        + (TOKEN,),
        (in_vmem(keep), in_vmem(came), in_vmem(token)),
        [VMEM] * 3,
    )


def gather_kernel(keep_ref, first_ref, second_ref, third_ref, token_ref, next_ref, send_ref, done_ref):
    half = next_ref.shape[0]
    total = keep_ref[...] + first_ref[...].astype(jnp.float32)
    total += second_ref[...].astype(jnp.float32) + third_ref[...].astype(jnp.float32)
    next_ref[...] = total[:half]
    send_ref[...] = total[half:].astype(send_ref.dtype)
    done_ref[...] = token_ref[...]


def gather(keep, came, token):
    rows, width = keep.shape
    return call(
        gather_kernel,
        "gather",
        (
            pltpu.VMEM((rows // 2, width), jnp.float32),
            pltpu.VMEM((rows // 2, width), jnp.bfloat16),
            TOKEN,
        ),
        (in_vmem(keep),) + tuple(in_vmem(c) for c in came) + (in_vmem(token),),
        [VMEM] * 5,
    )


def close_kernel(
    experts, keep_ref, first_ref, second_ref, third_ref, residual_ref, routes_ref, gates_ref,
    token_ref, total_ref, send_ref, done_ref,
):
    done_ref[...] = token_ref[...]
    per, width = residual_ref.shape
    total = keep_ref[...] + first_ref[...].astype(jnp.float32)
    total += second_ref[...].astype(jnp.float32) + third_ref[...].astype(jnp.float32)
    own = total[:per] + residual_ref[...].astype(jnp.float32)
    total = jnp.concatenate([own, total[per:]], axis=0)
    lane = lax.broadcasted_iota(jnp.int32, (per, TABLE), 1)
    routes, gates = routes_ref[...], gates_ref[...]
    table = jnp.zeros((per, TABLE), jnp.float32)
    for t in range(routes.shape[1]):
        table += jnp.where(routes[:, t : t + 1] == lane % experts, gates[:, t : t + 1], 0.0)
    high = table.astype(jnp.bfloat16).astype(jnp.float32)
    middle = (table - high).astype(jnp.bfloat16).astype(jnp.float32)
    low = table - high - middle
    part = lane // experts
    table = jnp.where(
        part == 0, high, jnp.where(part == 1, middle, jnp.where(part == 2, low, 0.0))
    )
    table = jnp.concatenate([table, jnp.zeros_like(table)], axis=0)
    total_ref[:, :width] = total
    total_ref[:, width:] = table
    send_ref[:, :width] = total.astype(send_ref.dtype)
    send_ref[:, width:] = table.astype(send_ref.dtype)


def close(keep, came, residual, routes, gates, token, experts):
    rows, width = keep.shape
    shape = (rows, width + TABLE)
    return call(
        functools.partial(close_kernel, experts),
        "close",
        (pltpu.VMEM(shape, jnp.float32), pltpu.VMEM(shape, jnp.bfloat16), TOKEN),
        (in_vmem(keep),)
        + tuple(in_vmem(c) for c in came)
        + (residual, routes, gates, in_vmem(token)),
        [VMEM] * 8,
    )


def norm_kernel(total_ref, came_ref, gain_ref, token_ref, attended_ref, normed_ref, done_ref):
    done_ref[...] = token_ref[...]
    per, width = attended_ref.shape
    came = came_ref[...].astype(jnp.float32)
    total = total_ref[...] + jnp.concatenate([came[per:], came[:per]], axis=0)
    attended = total[:, :width].astype(jnp.bfloat16).astype(jnp.float32)
    attended_ref[...] = attended[:per].astype(jnp.bfloat16)
    mean = jnp.mean(attended * attended, axis=1, keepdims=True)
    normed = attended * lax.rsqrt(mean + 1e-06) * gain_ref[...]
    normed_ref[:, :width] = normed.astype(jnp.bfloat16)
    normed_ref[:, width:] = total[:, width:].astype(jnp.bfloat16)


def norm(total, came, gain, token, per):
    rows, width = total.shape
    return call(
        norm_kernel,
        "norm",
        (
            pltpu.VMEM((per, width - TABLE), jnp.bfloat16),
            pltpu.VMEM((rows, width), jnp.bfloat16),
            TOKEN,
        ),
        (in_vmem(total), in_vmem(came), gain.reshape(1, -1), in_vmem(token)),
        [VMEM] * 4,
    )


def expert_kernel(blocks, experts, me_ref, *refs):
    gate, up, *firsts, down_hbm, token_ref, keep_ref, send_ref, done_ref, down, sems = refs[blocks:]
    early = sum(first.shape[1] for first in firsts)
    source = down_hbm.at[:, pl.ds(early, down.shape[1])]
    load = functools.partial(column_copy, source, down, sems)
    start_all(sems.shape[0], load)
    done_ref[...] = token_ref[...]
    model, units = gate.shape
    tile = down.shape[1] // sems.shape[0]
    half = keep_ref.shape[0]
    x = jnp.concatenate([r[...].astype(jnp.float32) for r in refs[:blocks]], axis=0)
    x = x.astype(jnp.bfloat16)
    table = x[:, model:].astype(jnp.float32)
    lane = lax.broadcasted_iota(jnp.int32, table.shape, 1)
    expert = (me_ref[0] * units) // FF_WIN
    mine = (lane % experts == expert) & (lane < 3 * experts)
    weight = jnp.sum(jnp.where(mine, table, 0.0), axis=1, keepdims=True)
    x = x[:, :model]
    rows = x.shape[0]
    x = tall(x)
    g = jnp.dot(x, gate[...], preferred_element_type=jnp.float32)[:rows]
    u = jnp.dot(x, up[...], preferred_element_type=jnp.float32)[:rows]
    act = tall((g / (1.0 + jnp.exp(-g)) * u).astype(jnp.bfloat16))

    def multiply(weights, at, to):
        y = jnp.dot(act, weights[:, at : at + tile], preferred_element_type=jnp.float32)
        y = y[:rows] * weight
        keep_ref[:, to : to + tile] = y[:half]
        send_ref[:, to : to + tile] = y[half:].astype(send_ref.dtype)

    to = 0
    for first in firsts:
        for t in range(0, first.shape[1], tile):
            multiply(first, t, to + t)
        to += first.shape[1]
    for i in range(sems.shape[0]):
        load(i).wait()
        multiply(down, i * tile, early + i * tile)


def expert(me, blocks, gate, up, firsts, down, token, experts):
    model, units = gate.shape
    half = sum(b.shape[0] for b in blocks) // 2
    late = model - sum(first.shape[1] for first in firsts)
    return call(
        functools.partial(expert_kernel, len(blocks), experts),
        "expert",
        (
            pltpu.VMEM((half, model), jnp.float32),
            pltpu.VMEM((half, model), jnp.bfloat16),
            TOKEN,
        ),
        (me,)
        + tuple(in_vmem(b) for b in blocks)
        + tuple(in_vmem(w) for w in (gate, up, *firsts))
        + (in_hbm(down), in_vmem(token)),
        [SMEM] + [VMEM] * (len(blocks) + 2 + len(firsts)) + [HBM, VMEM],
        [
            pltpu.VMEM((units, late), down.dtype),
            pltpu.SemaphoreType.DMA((late // tile_of(late, 1024),)),
        ],
        limit=10,
    )


def last_kernel(keep_ref, came_ref, token_ref, out_ref):
    out_ref[...] = (keep_ref[...] + came_ref[...].astype(jnp.float32)).astype(out_ref.dtype)


def body(
    queries,
    latent_key_cache,
    lengths,
    value_up_weight,
    out_proj,
    residual_in,
    norm_gain,
    w_gate,
    w_up,
    w_down,
    routes,
    route_gates,
):
    devices = lax.axis_size("exp")
    bits = devices.bit_length() - 1
    per = queries.shape[0]
    experts = devices * w_gate.shape[1] // FF_WIN
    me = lax.axis_index("exp").astype(jnp.int32).reshape(1)

    def swap(x, *some_bits):
        mask = sum(1 << bit for bit in some_bits)
        return lax.ppermute(x, "exp", [(i, i ^ mask) for i in range(devices)])

    def square(sends):
        low, high = bits - 3, bits - 2
        return swap(sends[0], high), swap(sends[1], low), swap(sends[2], low, high)

    early = out_proj.shape[1] // 7 * 2
    token = jnp.zeros(TOKEN.shape, TOKEN.dtype)
    latent, first = attend(me, queries, latent_key_cache, lengths, out_proj, early, bits)
    latent = lax.all_to_all(latent, "exp", split_axis=0, concat_axis=0, tiled=True)
    latents = [latent.reshape(-1, LATENT_WIDTH)]
    keep, send = project(me, latents, value_up_weight, out_proj, first, per, bits)
    for bit in range(bits - 4):
        keep, send, token = fold(keep, swap(send, bit), token)
    keep, *sends, token = fold(keep, swap(send, bits - 4), token, 4)
    came = square(sends)
    part = w_down.shape[1] // 7
    first, token = load(token, w_down, 2 * part)
    total, send, token = close(keep, came, residual_in, routes, route_gates, token, experts)
    came = swap(send, bits - 1)
    second, token = load(token, w_down, 2 * part, 2 * part)
    attended, x, token = norm(total, came, norm_gain, token, per)
    for bit in reversed(range(bits - 1)):
        if bit > 2:
            x = jnp.concatenate([x, swap(x, bit)], axis=0)
        elif bit == 2:
            blocks = [x, swap(x, 2), swap(x, 1), swap(x, 2, 1)]
        elif bit == 0:
            blocks = blocks + [swap(b, 0) for b in blocks]
    keep, send, token = expert(me, blocks, w_gate, w_up, [first, second], w_down, token, experts)
    for bit in range(bits - 4):
        keep, send, token = fold(keep, swap(send, bit), token)
    keep, *sends, token = fold(keep, swap(send, bits - 4), token, 4)
    keep, send, token = gather(keep, square(sends), token)
    (mixed,) = call(
        last_kernel,
        "last",
        (jax.ShapeDtypeStruct(attended.shape, jnp.bfloat16),),
        (in_vmem(keep), in_vmem(swap(send, bits - 1)), in_vmem(token)),
        [VMEM] * 3,
    )
    return attended, mixed


def solution(mesh):
    placed = (
        P(("grp", "exp"), None, None),
        P(("grp", "exp"), None, None),
        P(("grp", "exp")),
        P("exp", None, None),
        P("exp", None),
        P(("grp", "exp"), None),
        P(),
        P(None, "exp"),
        P(None, "exp"),
        P("exp", None),
        P(("grp", "exp"), None),
        P(("grp", "exp"), None),
    )
    return jax.shard_map(
        body,
        mesh=mesh,
        in_specs=placed,
        out_specs=(P(("grp", "exp"), None), P(("grp", "exp"), None)),
        check_vma=False,
    )
```

```python
import functools

import jax
import jax.numpy as jnp
from jax import lax
from jax.experimental import pallas as pl
from jax.experimental.pallas import tpu as pltpu
from jax.sharding import PartitionSpec as P

LATENT_WIDTH = 512
ROTARY_WIDTH = 64
HEAD_VALUE_WIDTH = 128
FF_WIN = 1024
TABLE = 128
MIB = 1 << 20

HBM = pl.BlockSpec(memory_space=pl.ANY)
VMEM = pl.BlockSpec(memory_space=pltpu.VMEM)
SMEM = pl.BlockSpec(memory_space=pltpu.SMEM)


def tile_of(extent, wanted):
    while extent % wanted:
        wanted //= 2
    return wanted


def in_hbm(x):
    return pltpu.with_memory_space_constraint(x, pltpu.HBM)


def in_vmem(x):
    return pltpu.with_memory_space_constraint(x, pltpu.VMEM)


TOKEN = pltpu.VMEM((8, 128), jnp.float32)


def tall(x):
    rows = x.shape[0]
    if rows >= 128:
        return x
    return jnp.concatenate([x, jnp.zeros((128 - rows, x.shape[1]), x.dtype)], axis=0)


def call(kernel, name, outs, ins, specs, scratch=(), limit=4, moved=None):
    cost = None
    if moved:
        cost = pl.CostEstimate(flops=0, bytes_accessed=moved, transcendentals=0)
    return pl.pallas_call(
        kernel,
        out_shape=outs,
        in_specs=specs,
        out_specs=tuple(VMEM for _ in outs),
        scratch_shapes=list(scratch),
        compiler_params=pltpu.CompilerParams(vmem_limit_bytes=limit * MIB),
        cost_estimate=cost,
        name=name,
    )(*ins)


def row_copy(source, target, sems, i):
    rows = source.shape[0] // sems.shape[0]
    at = pl.ds(pl.multiple_of(i * rows, rows), rows)
    return pltpu.make_async_copy(source.at[at], target.at[at], sems.at[i])


def column_copy(source, target, sems, i):
    tile = source.shape[1] // sems.shape[0]
    at = pl.ds(pl.multiple_of(i * tile, tile), tile)
    return pltpu.make_async_copy(source.at[:, at], target.at[:, at], sems.at[i])


def start_all(count, copy):
    def step(i, carry):
        copy(i).start()
        return carry

    lax.fori_loop(0, count, step, 0)


LOADS = 4


def load_kernel(start, token_ref, source, target, done_ref, sems):
    source = source.at[:, pl.ds(start, target.shape[1])]
    copies = [row_copy(source, target, sems, part) for part in range(LOADS)]
    for c in copies:
        c.start()
    done_ref[...] = token_ref[...]
    for c in copies:
        c.wait()


def load(token, weight, columns, start=0):
    return call(
        functools.partial(load_kernel, start),
        "load",
        (pltpu.VMEM((weight.shape[0], columns), weight.dtype), TOKEN),
        (in_vmem(token), in_hbm(weight)),
        [VMEM, HBM],
        [pltpu.SemaphoreType.DMA((LOADS,))],
        limit=2,
        moved=weight.shape[0] * columns * 2,
    )


def attend_kernel(
    bits, me_ref, lengths_hbm, q_hbm, cache_hbm, proj_hbm, *refs
):
    *outs, proj, lengths, queries, cache, sems, small_sems, proj_sems = refs
    load = functools.partial(
        row_copy, proj_hbm.at[:, pl.ds(0, proj.shape[1])], proj, proj_sems
    )
    requests, width, length = cache.shape
    chunks = sems.shape[1]
    chunk = length // chunks
    latent = outs[0].shape[-1]
    heads = queries.shape[2]
    here = heads >> bits
    scale = (HEAD_VALUE_WIDTH + ROTARY_WIDTH) ** (-0.5)

    def copy(r, c):
        at = pl.ds(pl.multiple_of(c * chunk, chunk), chunk)
        return pltpu.make_async_copy(
            cache_hbm.at[r, :, at], cache.at[r, :, at], sems.at[r, c]
        )

    first = [
        pltpu.make_async_copy(lengths_hbm, lengths, small_sems.at[0]),
        pltpu.make_async_copy(q_hbm, queries, small_sems.at[1]),
    ]
    for c in first:
        c.start()
    for r in range(requests):
        start_all(chunks, functools.partial(copy, r))
    for c in first:
        c.wait()
    order = one_hot(row_order(None, heads, here, bits))
    scores = []
    for r in range(requests):
        q = lax.dot_general(
            order,
            queries[r],
            (((1,), (1,)), ((), ())),
            preferred_element_type=jnp.float32,
        ).astype(jnp.bfloat16)
        parts = []
        for c in range(chunks):
            copy(r, c).wait()
            if r == 0 and c == chunks - 1:
                start_all(LOADS, load)
            s = jnp.dot(
                q,
                cache[r, :, c * chunk : (c + 1) * chunk],
                preferred_element_type=jnp.float32,
            )
            at = lax.broadcasted_iota(jnp.int32, s.shape, 1) + c * chunk
            parts.append(jnp.where(at < lengths[r], s * scale, -jnp.inf))
        scores.append(jnp.concatenate(parts, axis=1))
    results = []
    for r in range(requests):
        peak = jnp.max(scores[r], axis=1, keepdims=True)
        e = jnp.exp(scores[r] - peak)
        p = (e * (1.0 / jnp.sum(e, axis=1, keepdims=True))).astype(jnp.bfloat16)
        o = lax.dot_general(
            p,
            cache[r, :latent, :],
            (((1,), (1,)), ((), ())),
            preferred_element_type=jnp.float32,
        )
        results.append(o.reshape(1 << bits, here, latent))
    out = jnp.concatenate(results, axis=1).astype(jnp.bfloat16)
    share = (1 << bits) // len(outs)
    for i, ref in enumerate(outs):
        ref[...] = out[i * share : (i + 1) * share]
    for i in range(LOADS):
        load(i).wait()


def attend(me, queries, cache, lengths, proj, early, bits):
    sides = 1
    requests, heads, width = queries.shape
    length = cache.shape[1]
    devices = 1 << bits
    slots = requests * heads // devices
    chunks = length // tile_of(length, 1024)
    return call(
        functools.partial(attend_kernel, bits),
        "attend",
        (
            pltpu.VMEM((devices // sides, slots, LATENT_WIDTH), jnp.bfloat16),
            pltpu.VMEM((proj.shape[0], early), proj.dtype),
        ),
        (
            me,
            in_hbm(lengths),
            in_hbm(jnp.swapaxes(queries, 1, 2)),
            in_hbm(jnp.swapaxes(cache, 1, 2)),
            in_hbm(proj),
        ),
        [SMEM] + [HBM] * 4,
        [
            pltpu.SMEM((requests,), jnp.int32),
            pltpu.VMEM((requests, width, heads), jnp.bfloat16),
            pltpu.VMEM((requests, width, length), jnp.bfloat16),
            pltpu.SemaphoreType.DMA((requests, chunks)),
            pltpu.SemaphoreType.DMA((2,)),
            pltpu.SemaphoreType.DMA((LOADS,)),
        ],
        limit=16,
    )


def relative(index, bits):
    out = jnp.zeros_like(index)
    for b in range(bits):
        out = out | (((index >> b) & 1) << (bits - 1 - b))
    return out


def row_order(me, rows, per, bits):
    i = lax.broadcasted_iota(jnp.int32, (rows, rows), 0)
    j = lax.broadcasted_iota(jnp.int32, (rows, rows), 1)
    if me is None:
        return i == j
    shift = per.bit_length() - 1
    owner = relative(i >> shift, bits) ^ me
    return j == (owner << shift) + (i & (per - 1))


def one_hot(order):
    return jnp.where(order, 1.0, 0.0).astype(jnp.bfloat16)


def project_kernel(
    bits, per, me_ref, up_ref, proj_hbm, first, *refs
):
    *latents, keep_ref, send_ref, rest, sems = refs
    tile = rest.shape[1] // sems.shape[0]
    early = first.shape[1]
    source = proj_hbm.at[:, pl.ds(early, rest.shape[1])]
    load = functools.partial(column_copy, source, rest, sems)
    start_all(sems.shape[0], load)
    heads, latent, value = up_ref.shape
    x = jnp.concatenate([ref[...] for ref in latents], axis=0)
    rows = x.shape[0] // heads
    half = rows // 2
    parts = []
    together = min(2, heads)
    for h in range(0, heads, together):
        up = jnp.concatenate([up_ref[h + i] for i in range(together)], axis=1)
        y = jnp.dot(x, up, preferred_element_type=jnp.float32)
        y = y.reshape(rows, heads, together * value)
        head = lax.broadcasted_iota(jnp.int32, y.shape, 1)
        lane = lax.broadcasted_iota(jnp.int32, y.shape, 2)
        parts.append(jnp.sum(jnp.where(head == h + lane // value, y, 0.0), axis=1))
    values = jnp.concatenate(parts, axis=1).astype(jnp.bfloat16)
    order = row_order(me_ref[0], rows, per, bits)
    values = jnp.dot(one_hot(order), values, preferred_element_type=jnp.float32).astype(jnp.bfloat16)
    values = tall(values)

    def multiply(weights, at, to):
        y = jnp.dot(values, weights[:, at : at + tile], preferred_element_type=jnp.float32)
        keep_ref[:, to : to + tile] = y[:half]
        send_ref[:, to : to + tile] = y[half:rows].astype(send_ref.dtype)

    for t in range(0, early, tile):
        multiply(first, t, t)
    for i in range(sems.shape[0]):
        load(i).wait()
        multiply(rest, i * tile, early + i * tile)


def project(me, latents, up, proj, first, per, bits):
    depth, width = proj.shape
    late = width - first.shape[1]
    half = sum(x.shape[0] for x in latents) // up.shape[0] // 2
    return call(
        functools.partial(project_kernel, bits, per),
        "project",
        (pltpu.VMEM((half, width), jnp.float32), pltpu.VMEM((half, width), jnp.bfloat16)),
        (me, in_vmem(up), in_hbm(proj), in_vmem(first)) + tuple(in_vmem(x) for x in latents),
        [SMEM, VMEM, HBM, VMEM] + [VMEM] * len(latents),
        [
            pltpu.VMEM((depth, late), proj.dtype),
            pltpu.SemaphoreType.DMA((late // tile_of(late, 512),)),
        ],
        limit=12,
        moved=100 * MIB,
    )


def fold_kernel(parts, keep_ref, came_ref, *refs):
    rows = keep_ref.shape[0] // parts
    outs = refs[len(refs) - parts - 1 :]
    total = keep_ref[...] + came_ref[...].astype(jnp.float32)
    outs[0][...] = total[:rows]
    for i in range(1, parts):
        outs[i][...] = total[i * rows : (i + 1) * rows].astype(outs[i].dtype)
    outs[parts][...] = refs[0][...]


def fold(keep, came, token, parts=2):
    rows, width = keep.shape
    return call(
        functools.partial(fold_kernel, parts),
        "fold",
        (pltpu.VMEM((rows // parts, width), jnp.float32),)
        + (pltpu.VMEM((rows // parts, width), jnp.bfloat16),) * (parts - 1)
        + (TOKEN,),
        (in_vmem(keep), in_vmem(came), in_vmem(token)),
        [VMEM] * 3,
    )


def gather_kernel(keep_ref, first_ref, second_ref, third_ref, token_ref, next_ref, send_ref, done_ref):
    half = next_ref.shape[0]
    total = keep_ref[...] + first_ref[...].astype(jnp.float32)
    total += second_ref[...].astype(jnp.float32) + third_ref[...].astype(jnp.float32)
    next_ref[...] = total[:half]
    send_ref[...] = total[half:].astype(send_ref.dtype)
    done_ref[...] = token_ref[...]


def gather(keep, came, token):
    rows, width = keep.shape
    return call(
        gather_kernel,
        "gather",
        (
            pltpu.VMEM((rows // 2, width), jnp.float32),
            pltpu.VMEM((rows // 2, width), jnp.bfloat16),
            TOKEN,
        ),
        (in_vmem(keep),) + tuple(in_vmem(c) for c in came) + (in_vmem(token),),
        [VMEM] * 5,
    )


def close_kernel(
    experts, keep_ref, first_ref, second_ref, third_ref, residual_ref, routes_ref, gates_ref,
    token_ref, total_ref, send_ref, done_ref,
):
    done_ref[...] = token_ref[...]
    per, width = residual_ref.shape
    total = keep_ref[...] + first_ref[...].astype(jnp.float32)
    total += second_ref[...].astype(jnp.float32) + third_ref[...].astype(jnp.float32)
    own = total[:per] + residual_ref[...].astype(jnp.float32)
    total = jnp.concatenate([own, total[per:]], axis=0)
    lane = lax.broadcasted_iota(jnp.int32, (per, TABLE), 1)
    routes, gates = routes_ref[...], gates_ref[...]
    table = jnp.zeros((per, TABLE), jnp.float32)
    for t in range(routes.shape[1]):
        table += jnp.where(routes[:, t : t + 1] == lane % experts, gates[:, t : t + 1], 0.0)
    high = table.astype(jnp.bfloat16).astype(jnp.float32)
    middle = (table - high).astype(jnp.bfloat16).astype(jnp.float32)
    low = table - high - middle
    part = lane // experts
    table = jnp.where(
        part == 0, high, jnp.where(part == 1, middle, jnp.where(part == 2, low, 0.0))
    )
    table = jnp.concatenate([table, jnp.zeros_like(table)], axis=0)
    total_ref[:, :width] = total
    total_ref[:, width:] = table
    send_ref[:, :width] = total.astype(send_ref.dtype)
    send_ref[:, width:] = table.astype(send_ref.dtype)


def close(keep, came, residual, routes, gates, token, experts):
    rows, width = keep.shape
    shape = (rows, width + TABLE)
    return call(
        functools.partial(close_kernel, experts),
        "close",
        (pltpu.VMEM(shape, jnp.float32), pltpu.VMEM(shape, jnp.bfloat16), TOKEN),
        (in_vmem(keep),)
        + tuple(in_vmem(c) for c in came)
        + (residual, routes, gates, in_vmem(token)),
        [VMEM] * 8,
    )


def norm_kernel(total_ref, came_ref, gain_ref, token_ref, attended_ref, normed_ref, done_ref):
    done_ref[...] = token_ref[...]
    per, width = attended_ref.shape
    came = came_ref[...].astype(jnp.float32)
    total = total_ref[...] + jnp.concatenate([came[per:], came[:per]], axis=0)
    attended = total[:, :width].astype(jnp.bfloat16).astype(jnp.float32)
    attended_ref[...] = attended[:per].astype(jnp.bfloat16)
    mean = jnp.mean(attended * attended, axis=1, keepdims=True)
    normed = attended * lax.rsqrt(mean + 1e-06) * gain_ref[...]
    normed_ref[:, :width] = normed.astype(jnp.bfloat16)
    normed_ref[:, width:] = total[:, width:].astype(jnp.bfloat16)


def norm(total, came, gain, token, per):
    rows, width = total.shape
    return call(
        norm_kernel,
        "norm",
        (
            pltpu.VMEM((per, width - TABLE), jnp.bfloat16),
            pltpu.VMEM((rows, width), jnp.bfloat16),
            TOKEN,
        ),
        (in_vmem(total), in_vmem(came), gain.reshape(1, -1), in_vmem(token)),
        [VMEM] * 4,
    )


def expert_kernel(blocks, experts, me_ref, *refs):
    gate, up, *firsts, down_hbm, token_ref, keep_ref, send_ref, done_ref, down, sems = refs[blocks:]
    early = sum(first.shape[1] for first in firsts)
    source = down_hbm.at[:, pl.ds(early, down.shape[1])]
    load = functools.partial(column_copy, source, down, sems)
    start_all(sems.shape[0], load)
    done_ref[...] = token_ref[...]
    model, units = gate.shape
    tile = down.shape[1] // sems.shape[0]
    half = keep_ref.shape[0]
    x = jnp.concatenate([r[...].astype(jnp.float32) for r in refs[:blocks]], axis=0)
    x = x.astype(jnp.bfloat16)
    table = x[:, model:].astype(jnp.float32)
    lane = lax.broadcasted_iota(jnp.int32, table.shape, 1)
    expert = (me_ref[0] * units) // FF_WIN
    mine = (lane % experts == expert) & (lane < 3 * experts)
    weight = jnp.sum(jnp.where(mine, table, 0.0), axis=1, keepdims=True)
    x = x[:, :model]
    rows = x.shape[0]
    x = tall(x)
    g = jnp.dot(x, gate[...], preferred_element_type=jnp.float32)[:rows]
    u = jnp.dot(x, up[...], preferred_element_type=jnp.float32)[:rows]
    act = tall((g / (1.0 + jnp.exp(-g)) * u).astype(jnp.bfloat16))

    def multiply(weights, at, to):
        y = jnp.dot(act, weights[:, at : at + tile], preferred_element_type=jnp.float32)
        y = y[:rows] * weight
        keep_ref[:, to : to + tile] = y[:half]
        send_ref[:, to : to + tile] = y[half:].astype(send_ref.dtype)

    to = 0
    for first in firsts:
        for t in range(0, first.shape[1], tile):
            multiply(first, t, to + t)
        to += first.shape[1]
    for i in range(sems.shape[0]):
        load(i).wait()
        multiply(down, i * tile, early + i * tile)


def expert(me, blocks, gate, up, firsts, down, token, experts):
    model, units = gate.shape
    half = sum(b.shape[0] for b in blocks) // 2
    late = model - sum(first.shape[1] for first in firsts)
    return call(
        functools.partial(expert_kernel, len(blocks), experts),
        "expert",
        (
            pltpu.VMEM((half, model), jnp.float32),
            pltpu.VMEM((half, model), jnp.bfloat16),
            TOKEN,
        ),
        (me,)
        + tuple(in_vmem(b) for b in blocks)
        + tuple(in_vmem(w) for w in (gate, up, *firsts))
        + (in_hbm(down), in_vmem(token)),
        [SMEM] + [VMEM] * (len(blocks) + 2 + len(firsts)) + [HBM, VMEM],
        [
            pltpu.VMEM((units, late), down.dtype),
            pltpu.SemaphoreType.DMA((late // tile_of(late, 1024),)),
        ],
        limit=10,
    )


def last_kernel(keep_ref, came_ref, token_ref, out_ref):
    out_ref[...] = (keep_ref[...] + came_ref[...].astype(jnp.float32)).astype(out_ref.dtype)


def body(
    queries,
    latent_key_cache,
    lengths,
    value_up_weight,
    out_proj,
    residual_in,
    norm_gain,
    w_gate,
    w_up,
    w_down,
    routes,
    route_gates,
):
    devices = lax.axis_size("exp")
    bits = devices.bit_length() - 1
    per = queries.shape[0]
    experts = devices * w_gate.shape[1] // FF_WIN
    me = lax.axis_index("exp").astype(jnp.int32).reshape(1)

    def swap(x, *some_bits):
        mask = sum(1 << bit for bit in some_bits)
        return lax.ppermute(x, "exp", [(i, i ^ mask) for i in range(devices)])

    def square(sends):
        low, high = bits - 3, bits - 2
        return swap(sends[0], high), swap(sends[1], low), swap(sends[2], low, high)

    early = out_proj.shape[1] // 7 * 3
    token = jnp.zeros(TOKEN.shape, TOKEN.dtype)
    latent, first = attend(me, queries, latent_key_cache, lengths, out_proj, early, bits)
    latent = lax.all_to_all(latent, "exp", split_axis=0, concat_axis=0, tiled=True)
    latents = [latent.reshape(-1, LATENT_WIDTH)]
    keep, send = project(me, latents, value_up_weight, out_proj, first, per, bits)
    for bit in range(bits - 4):
        keep, send, token = fold(keep, swap(send, bit), token)
    keep, *sends, token = fold(keep, swap(send, bits - 4), token, 4)
    came = square(sends)
    part = w_down.shape[1] // 7
    first, token = load(token, w_down, 2 * part)
    total, send, token = close(keep, came, residual_in, routes, route_gates, token, experts)
    came = swap(send, bits - 1)
    second, token = load(token, w_down, 2 * part, 2 * part)
    attended, x, token = norm(total, came, norm_gain, token, per)
    for bit in reversed(range(bits - 1)):
        if bit > 2:
            x = jnp.concatenate([x, swap(x, bit)], axis=0)
        elif bit == 2:
            blocks = [x, swap(x, 2), swap(x, 1), swap(x, 2, 1)]
        elif bit == 0:
            blocks = blocks + [swap(b, 0) for b in blocks]
    keep, send, token = expert(me, blocks, w_gate, w_up, [first, second], w_down, token, experts)
    for bit in range(bits - 4):
        keep, send, token = fold(keep, swap(send, bit), token)
    keep, *sends, token = fold(keep, swap(send, bits - 4), token, 4)
    keep, send, token = gather(keep, square(sends), token)
    (mixed,) = call(
        last_kernel,
        "last",
        (jax.ShapeDtypeStruct(attended.shape, jnp.bfloat16),),
        (in_vmem(keep), in_vmem(swap(send, bits - 1)), in_vmem(token)),
        [VMEM] * 3,
    )
    return attended, mixed


def solution(mesh):
    placed = (
        P(("grp", "exp"), None, None),
        P(("grp", "exp"), None, None),
        P(("grp", "exp")),
        P("exp", None, None),
        P("exp", None),
        P(("grp", "exp"), None),
        P(),
        P(None, "exp"),
        P(None, "exp"),
        P("exp", None),
        P(("grp", "exp"), None),
        P(("grp", "exp"), None),
    )
    return jax.shard_map(
        body,
        mesh=mesh,
        in_specs=placed,
        out_specs=(P(("grp", "exp"), None), P(("grp", "exp"), None)),
        check_vma=False,
    )
```
